256 devices in a mesh: seq: 32 (over z, y), head: 8 (over x, core).
Axes of the slice: x: 4, y: 4, z: 8, core: 2. Of those that a mesh axis runs over, the one named last changes fastest.
Arguments:
- queries: bfloat16 [8192, 4096], P(('seq', 'head')), may hold values from -6 to 6
- new_keys: bfloat16 [8192, 4096], P(('seq', 'head')), may hold values from -6 to 6
- new_values: bfloat16 [8192, 4096], P(('seq', 'head')), may hold values from -6 to 6
- attn_out: bfloat16 [8192, 4096], P(('seq', 'head')), may hold values from -6 to 6
- out_grad: bfloat16 [8192, 4096], P(('seq', 'head')), may hold values from -384 to 384
- logsumexp: float32 [32, 8192], P('head', 'seq'), may hold values from 8 to 10
- ctx_keys: bfloat16 [65536, 4096], P('seq', 'head'), may hold values from -6 to 6
- ctx_values: bfloat16 [65536, 4096], P('seq', 'head'), may hold values from -6 to 6
- selected: int32 [32, 2], replicated, may hold values from 0 to 31, all different within a row; in each aligned block of 32 rows (0 to 31, 32 to 63, ...) at most 3 rows name the same one
Outputs:
- query_grad: bfloat16 [8192, 4096], P('seq', 'head')
- new_key_grad: bfloat16 [8192, 4096], P('seq', 'head')
- new_value_grad: bfloat16 [8192, 4096], P('seq', 'head')
- ctx_key_grad: bfloat16 [65536, 4096], P('seq', 'head')
- ctx_value_grad: bfloat16 [65536, 4096], P('seq', 'head')
The draws below stay inside these ranges and needn't reach their ends.
Inputs may be any that keep to these rules, and one draw needn't show every extreme that they name: Each row lists 2 different context blocks. Every context block is selected by at least one and at most 3 query blocks, and some block by exactly 3.
All inputs are finite; a program needn't handle non-finite values.
Results may differ from the reference program's by a relative error of at most 0.0058.
Values may be sent and summed in bfloat16 or wider, within the bound.
No kernel may reach another device: no remote copies, remote signals or barrier semaphores. Data moves between devices by JAX's collectives and lax.ppermute only.
A program may use at most 128 MiB of HBM per device.

```python
import math
import jax
import jax.numpy as jnp
import numpy as np
from jax import lax

HEADS = 32
DH = 128
QBLK = 256
KBLK = 2048
SEL = 2
CAP = 3
HIDDEN_SIZE = 4096
QBLOCKS = 32
QTOK = 8192
CTX_BLOCKS = 32
CTX_TOK = 65536


def steps_of(rng, shape, pieces, low, largest):
    factor_of = 1.0
    for axis_at, shards_of in pieces:
        steps = jax.random.uniform(jax.random.fold_in(jax.random.fold_in(rng, 6), axis_at), (shards_of,), jnp.float32, low / len(pieces), largest / len(pieces))
        factor_of = factor_of * jnp.repeat(jnp.exp(steps), shape[axis_at] // shards_of).reshape((-1,) + (1,) * (len(shape) - 1 - axis_at))
    return factor_of


def shared_out(stream_key, own, number, rows, amount, top, most, lean):
    ranking = jax.random.permutation(stream_key, amount)
    packed, ordinary = shares(amount, rows * top, most, lean, True), shares(amount, rows * top, most, lean, False)
    places = jnp.arange(amount)

    def named(sizes, offset_by):
        used = int((sizes > 0).sum())
        fixed = max(1, used // 4)
        shifted = fixed + (places - fixed + offset_by * (used - fixed)) % max(1, amount - fixed)
        return jnp.zeros((amount,), jnp.int32).at[ranking[jnp.where(places < fixed, places, shifted)]].set(jnp.asarray(sizes, jnp.int32))

    sizes = jnp.where(number % 4 == 0, named(packed, number // 4), named(ordinary, number - number // 4 - 1))
    mixed = jax.random.permutation(jax.random.fold_in(own, 3), amount)
    donor, receiver = mixed[0:amount // 2 * 2:2], mixed[1:amount // 2 * 2:2]
    room = jnp.minimum(sizes[donor] - 1, most - sizes[receiver]) // 2
    room = jnp.where((donor == ranking[0]) | (receiver == ranking[0]) | (sizes[receiver] == 0), 0, jnp.maximum(room, 0))
    shifted = jax.random.randint(jax.random.fold_in(own, 4), (amount // 2,), 0, 1 << 20) % (room + 1)
    sizes = sizes.at[donor].add(-shifted).at[receiver].add(shifted)
    labels = jnp.searchsorted(jnp.cumsum(sizes), jnp.arange(rows * top), side="right").astype(jnp.int32)
    table = labels.reshape(top, rows).T
    table = table[jax.random.permutation(jax.random.fold_in(own, 1), rows)]
    offset_by = jax.random.randint(jax.random.fold_in(own, 2), (rows, 1), 0, top)
    return jnp.take_along_axis(table, (jnp.arange(top)[None, :] + offset_by) % top, axis=1)


def shares(amount, total, reach, lean, full):
    portions = [(1 << 20) // math.isqrt(rank ** lean) + 1 for rank in range(1, amount + 1)]
    largest = reach if full else min(reach, max(-(-total // amount), total * portions[0] // sum(portions)))
    least = 1 if total - largest >= amount - 1 else 0
    counts, rest = [largest] + [least] * (amount - 1), total - largest - least * (amount - 1)
    while rest > 0:
        free = [i for i in range(1, amount) if counts[i] < largest] or [i for i in range(1, amount) if counts[i] < reach]
        mass, budget = sum([portions[i] for i in free]), rest
        for i in free:
            extra = min(reach - counts[i], max(1, budget * portions[i] // mass), rest)
            counts[i] = counts[i] + extra
            rest = rest - extra
    return np.array(counts)


def bell_draw(rng, dims, deviation, most, pieces=(), held_as=jnp.bfloat16):
    gain = steps_of(rng, dims, pieces, -0.22, 0.18) if pieces else 1.0
    array = jax.random.normal(rng, dims, jnp.float32) * deviation * gain
    return jnp.minimum(jnp.maximum(array, -most), most).astype(held_as)


def setup_inputs(seed: int = 0) -> dict:
    seeds = jax.random.split(jax.random.key(seed), 10)
    queries = bell_draw(seeds[0], (QTOK, HIDDEN_SIZE), 1.0, 6.0, ((0, 256),))
    new_keys = bell_draw(seeds[1], (QTOK, HIDDEN_SIZE), 1.0, 6.0, ((0, 256),))
    new_values = bell_draw(seeds[2], (QTOK, HIDDEN_SIZE), 1.0, 6.0, ((0, 256),))
    attn_out = bell_draw(seeds[3], (QTOK, HIDDEN_SIZE), 1.0, 6.0, ((0, 256),))
    out_grad = bell_draw(seeds[4], (QTOK, HIDDEN_SIZE), 64.0, 384.0, ((0, 256),))
    logsumexp = jnp.clip(8.0 + 2.0 * jax.random.uniform(seeds[5], (HEADS, QTOK), jnp.float32) ** steps_of(seeds[5], (HEADS, QTOK), ((0, 8), (1, 32)), -0.2, 0.2), 8.0, 10.0)
    ctx_keys = bell_draw(seeds[6], (CTX_TOK, HIDDEN_SIZE), 1.0, 6.0, ((0, 32), (1, 8)))
    ctx_values = bell_draw(seeds[7], (CTX_TOK, HIDDEN_SIZE), 1.0, 6.0, ((0, 32), (1, 8)))
    selected_keys = jax.random.split(jax.random.fold_in(seeds[8], 1), QBLOCKS // QBLOCKS)
    selected_turns = jax.random.permutation(jax.random.fold_in(seeds[8], 3), QBLOCKS // QBLOCKS)
    selected = jax.vmap(lambda own, number: shared_out(jax.random.fold_in(seeds[8], 2), own, number, QBLOCKS, CTX_BLOCKS, SEL, CAP, 2))(selected_keys, selected_turns).reshape((QBLOCKS, SEL))
    return dict(queries=queries, new_keys=new_keys, new_values=new_values, attn_out=attn_out, out_grad=out_grad, logsumexp=logsumexp, ctx_keys=ctx_keys, ctx_values=ctx_values, selected=selected)


def head_grads(query, key_block, value_block, grad_out, log_norm, out_dot, allowed):
    scaling = query.shape[-1] ** -0.5
    query_f = query.astype(jnp.float32)
    keys_f = key_block.astype(jnp.float32)
    values_f = value_block.astype(jnp.float32)
    grad_f = grad_out.astype(jnp.float32)
    scores = jnp.einsum('qhd,khd->hqk', query_f, keys_f) * scaling
    weights = jnp.exp(scores - log_norm[:, :, None])
    if allowed is not None:
        weights = jnp.where(allowed[None], weights, 0.0)
    rounded = lax.optimization_barrier(weights.astype(jnp.bfloat16)).astype(jnp.float32)
    value_part = jnp.einsum('hqk,qhd->khd', rounded, grad_f)
    dweights = jnp.einsum('qhd,khd->hqk', grad_f, values_f)
    dscores = weights * (dweights - out_dot[:, :, None])
    dscores = lax.optimization_barrier(dscores.astype(jnp.bfloat16)).astype(jnp.float32)
    query_part = jnp.einsum('hqk,khd->qhd', dscores, keys_f) * scaling
    key_part = jnp.einsum('hqk,qhd->khd', dscores, query_f) * scaling
    return query_part, key_part, value_part


def reference(queries, new_keys, new_values, attn_out, out_grad, logsumexp, ctx_keys, ctx_values, selected):
    def window_view(tensor):
        return tensor.reshape(QBLOCKS, QBLK, HEADS, DH)

    query_b = window_view(queries)
    keys_b = window_view(new_keys)
    values_b = window_view(new_values)
    grads_b = window_view(out_grad)
    log_b = logsumexp.reshape(HEADS, QBLOCKS, QBLK).transpose(1, 0, 2)
    products = out_grad.astype(jnp.float32) * attn_out.astype(jnp.float32)
    dots_b = jnp.sum(products.reshape(QBLOCKS, QBLK, HEADS, DH), axis=-1).transpose(0, 2, 1)
    context_k = ctx_keys.reshape(CTX_BLOCKS, KBLK, HEADS, DH)
    context_v = ctx_values.reshape(CTX_BLOCKS, KBLK, HEADS, DH)
    causal = jnp.arange(QBLK)[:, None] >= jnp.arange(QBLK)[None, :]

    def advance(totals, block_inputs):
        total_k, total_v = totals
        query, own_k, own_v, grad_out, log_norm, out_dot, chosen = block_inputs
        query_sum, own_dk, own_dv = head_grads(query, own_k, own_v, grad_out, log_norm, out_dot, causal)
        for slot in range(SEL):
            target = chosen[slot].astype(jnp.int32)
            block_k = lax.dynamic_index_in_dim(context_k, target, 0, keepdims=False)
            block_v = lax.dynamic_index_in_dim(context_v, target, 0, keepdims=False)
            part_q, part_k, part_v = head_grads(query, block_k, block_v, grad_out, log_norm, out_dot, None)
            query_sum = query_sum + part_q
            part_k = lax.optimization_barrier(part_k.astype(jnp.bfloat16)).astype(jnp.float32)
            part_v = lax.optimization_barrier(part_v.astype(jnp.bfloat16)).astype(jnp.float32)
            total_k = total_k.at[target].add(part_k)
            total_v = total_v.at[target].add(part_v)
        outputs = (query_sum.astype(jnp.bfloat16), own_dk.astype(jnp.bfloat16), own_dv.astype(jnp.bfloat16))
        return (total_k, total_v), outputs

    zeros = jnp.zeros((CTX_BLOCKS, KBLK, HEADS, DH), jnp.float32)
    finals, outputs = lax.scan(advance, (zeros, zeros), (query_b, keys_b, values_b, grads_b, log_b, dots_b, selected))
    query_grad = outputs[0].reshape(QTOK, HEADS * DH)
    new_key_grad = outputs[1].reshape(QTOK, HEADS * DH)
    new_value_grad = outputs[2].reshape(QTOK, HEADS * DH)
    ctx_key_grad = finals[0].reshape(CTX_TOK, HEADS * DH).astype(jnp.bfloat16)
    ctx_value_grad = finals[1].reshape(CTX_TOK, HEADS * DH).astype(jnp.bfloat16)
    return (query_grad, new_key_grad, new_value_grad, ctx_key_grad, ctx_value_grad)
```

```python
import functools
import math

import jax
import jax.numpy as jnp
from jax import lax
from jax.experimental import pallas as pl
from jax.experimental.pallas import tpu as pltpu
from jax.sharding import PartitionSpec as P

BF16 = jnp.bfloat16
F32 = jnp.float32
LANES = 128
VMEM_LIMIT = 48 * 1024 * 1024
SLOTS = 3
NT = (((1,), (1,)), ((), ()))
TN = (((0,), (0,)), ((), ()))
FILL = 1e5


def dot(lhs, rhs, dims=(((1,), (0,)), ((), ()))):
    return lax.dot_general(lhs, rhs, dims, preferred_element_type=F32)


def vmem():
    return pl.BlockSpec(memory_space=pltpu.VMEM)


def params():
    return pltpu.CompilerParams(vmem_limit_bytes=VMEM_LIMIT)


def spread_terms(rows):
    high = rows.astype(BF16)
    rest = rows - high.astype(F32)
    middle = rest.astype(BF16)
    low = (rest - middle.astype(F32)).astype(BF16)
    shape = (rows.shape[1], LANES)
    at = lax.broadcasted_iota(jnp.int32, shape, 0)
    lane = lax.broadcasted_iota(jnp.int32, shape, 1)
    out = jnp.zeros((rows.shape[0], LANES), F32)
    for term, values in enumerate((high, middle, low)):
        pick = jnp.where(lane == at * 4 + term, 1.0, 0.0).astype(BF16)
        out = out + dot(values, pick)
    return out


def prepare_kernel(q_ref, do_ref, o_ref, lse_ref, out_ref, lse_out_ref):
    rows, features = q_ref.shape
    heads = features // LANES
    groups = out_ref.shape[0]
    per_group = heads // groups
    product = do_ref[...].astype(F32) * o_ref[...].astype(F32)
    high = product.astype(BF16)
    low = (product - high.astype(F32)).astype(BF16)
    head_at = lax.broadcasted_iota(jnp.int32, (heads, features), 0)
    lane = lax.broadcasted_iota(jnp.int32, (heads, features), 1)
    pick = jnp.where((lane >= head_at * LANES) & (lane < head_at * LANES + LANES), 1.0, 0.0).astype(BF16)
    dots = dot(pick, high, NT) + dot(pick, low, NT)
    dot_terms = spread_terms(dots)
    for h in range(groups):
        for g in range(per_group):
            c = (h * per_group + g) * LANES
            out_ref[h, g * rows : (g + 1) * rows, :] = q_ref[:, c : c + LANES]
            base = (per_group + g) * rows
            out_ref[h, base : base + rows, :] = do_ref[:, c : c + LANES]
        block = dot_terms[h * per_group : (h + 1) * per_group]
        block = jnp.concatenate([block, jnp.zeros((8 - per_group, LANES), F32)], axis=0)
        out_ref[h, 2 * per_group * rows :, :] = block.astype(BF16)
    lse_out_ref[...] = spread_terms(lse_ref[...] * math.sqrt(LANES)).astype(BF16)


def relay_kernel(h_ref, lse_ref, out_ref):
    groups = h_ref.shape[0]
    per_group = lse_ref.shape[0] // groups
    rows = 32
    lse = lse_ref[...].astype(F32)
    quarters = groups // 2
    for g in range(per_group):
        for u in range(quarters):
            for a in range(2):
                r = (a * per_group + g) * quarters + u
                base = (a * per_group + g) * rows
                stats = []
                for part in range(2):
                    src = 2 * u + part
                    out_ref[r, part * rows : (part + 1) * rows, :] = h_ref[src, base : base + rows, :]
                    if a == 0:
                        stats.append(lse[g * groups + src : g * groups + src + 1])
                    else:
                        tile = h_ref[src, 2 * per_group * rows :, :].astype(F32)
                        stats.append(tile[g : g + 1])
                stats.append(jnp.zeros((6, LANES), F32))
                out_ref[r, 2 * rows :, :] = jnp.concatenate(stats, axis=0).astype(BF16)


def gather_kernel(src_ref, fill_ref, in_ref, out_ref):
    owners = out_ref.shape[0]
    fill = fill_ref[0].astype(F32)

    def body(j, carry):
        stats = []
        for slot in range(SLOTS):
            src = src_ref[j * SLOTS + slot]
            at = jnp.maximum(src, 0)
            out_ref[j, slot * 64 : (slot + 1) * 64, :] = in_ref[at, 0:64, :]
            tile = in_ref[at, 64:72, :].astype(F32)
            stats.append(jnp.where(src >= 0, tile[0:2], fill))
        stats.append(jnp.zeros((8 - 2 * SLOTS, LANES), F32))
        out_ref[j, SLOTS * 64 :, :] = jnp.concatenate(stats, axis=0).astype(BF16)
        return carry

    lax.fori_loop(0, owners, body, 0)


def term_mask():
    row = lax.broadcasted_iota(jnp.int32, (32, LANES), 0)
    lane = lax.broadcasted_iota(jnp.int32, (32, LANES), 1)
    return (lane >= row * 4) & (lane < row * 4 + 4)


def assemble(x_ref, head, qx, dx):
    mask = term_mask()
    for a, out in ((0, qx), (1, dx)):
        for u in range(4):
            r = a * 16 + head * 4 + u
            stats = x_ref[r, SLOTS * 64 :, :].astype(F32)
            for slot in range(SLOTS):
                base = slot * 256 + u * 64
                out[base : base + 64, 0:LANES] = x_ref[r, slot * 64 : (slot + 1) * 64, :]
                for part in range(2):
                    row = slot * 2 + part
                    ext = jnp.where(mask, stats[row : row + 1], 0.0).astype(BF16)
                    out[base + part * 32 : base + part * 32 + 32, LANES:] = ext


def extend(block):
    return jnp.concatenate([block, jnp.full((block.shape[0], LANES), -1.0, BF16)], axis=1)


SCALE = LANES**-0.5
EXP_SCALE = SCALE * math.log2(math.e)


def query_kernel(x_ref, k_ref, v_ref, out_ref, qx, dx, acc, *, chunk):
    head = pl.program_id(0)
    assemble(x_ref, head, qx, dx)
    acc[...] = jnp.zeros_like(acc)

    def body(i, carry):
        at = pl.ds(pl.multiple_of(i * chunk, chunk), chunk)
        keys = k_ref[at, :]
        weights = jnp.exp2(dot(qx[...], extend(keys), NT) * EXP_SCALE)
        dscores = (weights * dot(dx[...], extend(v_ref[at, :]), NT)).astype(BF16)
        acc[...] += dot(dscores, keys)
        return carry

    lax.fori_loop(0, k_ref.shape[0] // chunk, body, 0)
    for e in range(8):
        for slot in range(SLOTS):
            base = slot * 256 + e * 32
            out_ref[e, slot * 32 : (slot + 1) * 32, :] = (acc[base : base + 32, :] * SCALE).astype(BF16)


def context_kernel(x_ref, k_ref, v_ref, dk_ref, dv_ref, qx, dx, *, chunk):
    head = pl.program_id(0)
    assemble(x_ref, head, qx, dx)

    def body(i, carry):
        at = pl.ds(pl.multiple_of(i * chunk, chunk), chunk)
        weights = jnp.exp2(dot(extend(k_ref[at, :]), qx[...], NT) * EXP_SCALE)
        dscores = (weights * dot(extend(v_ref[at, :]), dx[...], NT)).astype(BF16)
        dv_ref[at, :] = dot(weights.astype(BF16), dx[:, 0:LANES]).astype(BF16)
        dk_ref[at, :] = (dot(dscores, qx[:, 0:LANES]) * SCALE).astype(BF16)
        return carry

    lax.fori_loop(0, k_ref.shape[0] // chunk, body, 0)


def own_kernel(h_ref, kv_ref, lse_ref, dq_ref, dk_ref, dv_ref, qx, dx, kx, vx):
    head = pl.program_id(0)
    groups = h_ref.shape[0]
    mask = term_mask()
    lse = lse_ref[0].astype(F32)
    kx[:, LANES:] = jnp.full((kx.shape[0], LANES), -1.0, BF16)
    vx[:, LANES:] = jnp.full((kx.shape[0], LANES), -1.0, BF16)
    for src in range(groups):
        at = slice(src * 32, src * 32 + 32)
        first = pl.ds(pl.multiple_of(head * 32, 32), 32)
        second = pl.ds(pl.multiple_of(head * 32 + 128, 32), 32)
        qx[at, 0:LANES] = h_ref[src, first, :]
        dx[at, 0:LANES] = h_ref[src, second, :]
        kx[at, 0:LANES] = kv_ref[src, first, :]
        vx[at, 0:LANES] = kv_ref[src, second, :]
        qx[at, LANES:] = jnp.where(mask, lse[src : src + 1], 0.0).astype(BF16)
        tile = h_ref[src, 256:, :].astype(F32)
        at_head = lax.broadcasted_iota(jnp.int32, tile.shape, 0) == head
        row = jnp.sum(jnp.where(at_head, tile, 0.0), axis=0, keepdims=True)
        dx[at, LANES:] = jnp.where(mask, row, 0.0).astype(BF16)
    shape = (qx.shape[0], kx.shape[0])
    allowed = lax.broadcasted_iota(jnp.int32, shape, 0) >= lax.broadcasted_iota(jnp.int32, shape, 1)
    weights = jnp.where(allowed, jnp.exp2(dot(qx[...], kx[...], NT) * EXP_SCALE), 0.0)
    dscores = (weights * dot(dx[...], vx[...], NT)).astype(BF16)
    dq_ref[...] = dot(dscores, kx[:, 0:LANES]) * SCALE
    dk_ref[...] = (dot(dscores, qx[:, 0:LANES], TN) * SCALE).astype(BF16)
    dv_ref[...] = dot(weights.astype(BF16), dx[:, 0:LANES], TN).astype(BF16)


def pair_kernel(at_ref, in_ref, out_ref):
    def body(b, carry):
        total = None
        for s in range(2):
            part = at_ref[b * 2 + s]
            owner = part // SLOTS
            row = pl.multiple_of((part - owner * SLOTS) * 32, 32)
            value = in_ref[owner, pl.ds(row, 32), :].astype(F32)
            total = value if total is None else total + value
        out_ref[b] = total.astype(BF16)
        return carry

    lax.fori_loop(0, out_ref.shape[0], body, 0)


def finish_kernel(in_ref, own_ref, out_ref):
    out_ref[...] = (in_ref[...].astype(F32).reshape(own_ref.shape) + own_ref[...]).astype(BF16)


def per_device(queries, new_keys, new_values, attn_out, out_grad, logsumexp, ctx_keys, ctx_values, selected):
    owners = lax.axis_size("seq")
    groups = lax.axis_size("head")
    per_group, block_rows = logsumexp.shape
    rows = queries.shape[0]
    key_rows, features = ctx_keys.shape
    relay = lax.axis_index("seq")

    flat = selected.reshape(-1)
    order = jnp.arange(flat.shape[0])
    same = flat[:, None] == flat[None, :]
    slot_of = jnp.sum(same & (order[None, :] < order[:, None]), axis=1).astype(jnp.int32)
    place = flat * SLOTS + slot_of
    hit = place[None, :] == jnp.arange(owners * SLOTS)[:, None]
    source = jnp.max(jnp.where(hit, (order // selected.shape[1])[None, :], -1), axis=1).astype(jnp.int32)
    fill = jnp.where(relay < owners // 2, FILL, 0.0).astype(F32).reshape(1)

    lse_rows = logsumexp.reshape(per_group * groups, rows)
    head_out, lse_terms = pl.pallas_call(
        prepare_kernel,
        out_shape=(
            jax.ShapeDtypeStruct((groups, 2 * per_group * rows + 8, LANES), BF16),
            jax.ShapeDtypeStruct((per_group * groups, LANES), BF16),
        ),
        in_specs=[vmem()] * 4,
        out_specs=(vmem(), vmem()),
        compiler_params=params(),
        name="prepare",
    )(queries, out_grad, attn_out, lse_rows)
    window = lax.all_to_all(head_out, "head", split_axis=0, concat_axis=0, tiled=True)

    pieces = pl.pallas_call(
        relay_kernel,
        out_shape=jax.ShapeDtypeStruct((owners, 72, LANES), BF16),
        in_specs=[vmem()] * 2,
        out_specs=vmem(),
        compiler_params=params(),
        name="relay",
    )(window, lse_terms)
    held = lax.all_to_all(pieces, "seq", split_axis=0, concat_axis=0, tiled=True)

    smem = pl.BlockSpec(memory_space=pltpu.SMEM)
    outgoing = pl.pallas_call(
        gather_kernel,
        out_shape=jax.ShapeDtypeStruct((owners, SLOTS * 64 + 8, LANES), BF16),
        in_specs=[smem, smem, vmem()],
        out_specs=vmem(),
        compiler_params=params(),
        name="gather",
    )(source, fill, held)
    items = lax.all_to_all(outgoing, "seq", split_axis=0, concat_axis=0, tiled=True)

    def heads_of(tensor):
        return tensor.reshape(rows, groups, per_group, LANES).transpose(1, 2, 0, 3).reshape(groups, per_group * rows, LANES)

    own_kv = jnp.concatenate([heads_of(new_keys), heads_of(new_values)], axis=1)
    items, own_kv = lax.optimization_barrier((items, own_kv))
    own_kv = lax.all_to_all(own_kv, "head", split_axis=0, concat_axis=0, tiled=True)

    chunk = 256
    slot_rows = SLOTS * block_rows
    context_spec = pl.BlockSpec((key_rows, LANES), lambda g: (0, g))
    items_spec = pl.BlockSpec((owners, SLOTS * 64 + 8, LANES), lambda g: (0, 0, 0))
    work = 2 * slot_rows * key_rows * LANES * per_group
    parts = pl.pallas_call(
        functools.partial(query_kernel, chunk=chunk),
        grid=(per_group,),
        out_shape=jax.ShapeDtypeStruct((owners, SLOTS * 32, LANES), BF16),
        in_specs=[items_spec, context_spec, context_spec],
        out_specs=pl.BlockSpec((owners // per_group, SLOTS * 32, LANES), lambda g: (g, 0, 0)),
        scratch_shapes=[
            pltpu.VMEM((slot_rows, 2 * LANES), BF16),
            pltpu.VMEM((slot_rows, 2 * LANES), BF16),
            pltpu.VMEM((slot_rows, LANES), F32),
        ],
        compiler_params=params(),
        cost_estimate=pl.CostEstimate(flops=5 * work, bytes_accessed=6 << 20, transcendentals=slot_rows * key_rows * per_group),
        name="query_parts",
    )(items, ctx_keys, ctx_values)

    returned = lax.all_to_all(parts, "seq", split_axis=0, concat_axis=0, tiled=True)

    items_later, own_kv, _ = lax.optimization_barrier((items, own_kv, parts))
    ctx_key_grad, ctx_value_grad = pl.pallas_call(
        functools.partial(context_kernel, chunk=chunk),
        grid=(per_group,),
        out_shape=(jax.ShapeDtypeStruct((key_rows, features), BF16),) * 2,
        in_specs=[items_spec, context_spec, context_spec],
        out_specs=(context_spec, context_spec),
        scratch_shapes=[
            pltpu.VMEM((slot_rows, 2 * LANES), BF16),
            pltpu.VMEM((slot_rows, 2 * LANES), BF16),
        ],
        compiler_params=params(),
        cost_estimate=pl.CostEstimate(flops=6 * work, bytes_accessed=10 << 20, transcendentals=slot_rows * key_rows * per_group),
        name="context_grads",
    )(items_later, ctx_keys, ctx_values)

    head_spec = pl.BlockSpec((block_rows, LANES), lambda g: (0, g))
    whole = lambda shape: pl.BlockSpec(shape, lambda g: (0,) * len(shape))
    own_dq, new_key_grad, new_value_grad = pl.pallas_call(
        own_kernel,
        grid=(per_group,),
        out_shape=(
            jax.ShapeDtypeStruct((block_rows, features), F32),
            jax.ShapeDtypeStruct((block_rows, features), BF16),
            jax.ShapeDtypeStruct((block_rows, features), BF16),
        ),
        in_specs=[whole(window.shape), whole(own_kv.shape), pl.BlockSpec((1, groups, LANES), lambda g: (g, 0, 0))],
        out_specs=(head_spec, head_spec, head_spec),
        scratch_shapes=[pltpu.VMEM((block_rows, 2 * LANES), BF16)] * 4,
        compiler_params=params(),
        cost_estimate=pl.CostEstimate(flops=10 * block_rows * block_rows * features, bytes_accessed=2 << 20, transcendentals=0),
        name="own_set",
    )(window, own_kv, lse_terms.reshape(per_group, groups, LANES))

    summed = pl.pallas_call(
        pair_kernel,
        out_shape=jax.ShapeDtypeStruct((owners, 32, LANES), BF16),
        in_specs=[smem, vmem()],
        out_specs=vmem(),
        compiler_params=params(),
        name="pair_sum",
    )(place, returned)
    home = lax.all_to_all(summed, "seq", split_axis=0, concat_axis=0, tiled=True)
    query_grad = pl.pallas_call(
        finish_kernel,
        grid=(per_group,),
        out_shape=jax.ShapeDtypeStruct((block_rows, features), BF16),
        in_specs=[pl.BlockSpec((owners // per_group, 32, LANES), lambda g: (g, 0, 0)), head_spec],
        out_specs=head_spec,
        compiler_params=params(),
        name="finish",
    )(home, own_dq)
    return (query_grad, new_key_grad, new_value_grad, ctx_key_grad, ctx_value_grad)


def solution(mesh):
    in_specs = (
        P(("seq", "head"), None),
        P(("seq", "head"), None),
        P(("seq", "head"), None),
        P(("seq", "head"), None),
        P(("seq", "head"), None),
        P("head", "seq"),
        P("seq", "head"),
        P("seq", "head"),
        P(),
    )
    out_specs = (P("seq", "head"),) * 5
    return jax.shard_map(per_device, mesh=mesh, in_specs=in_specs, out_specs=out_specs, check_vma=False)
```

```python
import functools
import math

import jax
import jax.numpy as jnp
from jax import lax
from jax.experimental import pallas as pl
from jax.experimental.pallas import tpu as pltpu
from jax.sharding import PartitionSpec as P

BF16 = jnp.bfloat16
F32 = jnp.float32
LANES = 128
MIB = 1024 * 1024
SLOTS = 3
NT = (((1,), (1,)), ((), ()))
TN = (((0,), (0,)), ((), ()))
FILL = 1e5


def dot(lhs, rhs, dims=(((1,), (0,)), ((), ()))):
    return lax.dot_general(lhs, rhs, dims, preferred_element_type=F32)


def vmem():
    return pl.BlockSpec(memory_space=pltpu.VMEM)


def in_hbm(array):
    return pltpu.with_memory_space_constraint(array, pltpu.HBM)


def params(mib=8):
    return pltpu.CompilerParams(vmem_limit_bytes=mib * MIB)


def spread_terms(rows):
    high = rows.astype(BF16)
    rest = rows - high.astype(F32)
    middle = rest.astype(BF16)
    low = (rest - middle.astype(F32)).astype(BF16)
    shape = (rows.shape[1], LANES)
    at = lax.broadcasted_iota(jnp.int32, shape, 0)
    lane = lax.broadcasted_iota(jnp.int32, shape, 1)
    out = jnp.zeros((rows.shape[0], LANES), F32)
    for term, values in enumerate((high, middle, low)):
        pick = jnp.where(lane == at * 4 + term, 1.0, 0.0).astype(BF16)
        out = out + dot(values, pick)
    return out


def lse_kernel(lse_ref, out_ref):
    out_ref[...] = spread_terms(lse_ref[...] * math.sqrt(LANES)).astype(BF16)


def prepare_kernel(q_hbm, do_hbm, o_hbm, out_ref, q_ref, do_ref, o_ref, sems):
    copies = [
        pltpu.make_async_copy(src, dst, sems.at[n])
        for n, (src, dst) in enumerate(((do_hbm, do_ref), (o_hbm, o_ref), (q_hbm, q_ref)))
    ]
    for copy in copies:
        copy.start()
    rows, features = q_ref.shape
    heads = features // LANES
    groups = out_ref.shape[0]
    per_group = heads // groups
    copies[0].wait()
    copies[1].wait()
    product = do_ref[...].astype(F32) * o_ref[...].astype(F32)
    high = product.astype(BF16)
    low = (product - high.astype(F32)).astype(BF16)
    head_at = lax.broadcasted_iota(jnp.int32, (heads, features), 0)
    lane = lax.broadcasted_iota(jnp.int32, (heads, features), 1)
    pick = jnp.where((lane >= head_at * LANES) & (lane < head_at * LANES + LANES), 1.0, 0.0).astype(BF16)
    dots = dot(pick, high, NT) + dot(pick, low, NT)
    dot_terms = spread_terms(dots)
    copies[2].wait()
    for h in range(groups):
        for g in range(per_group):
            c = (h * per_group + g) * LANES
            out_ref[h, g * rows : (g + 1) * rows, :] = q_ref[:, c : c + LANES]
            base = (per_group + g) * rows
            out_ref[h, base : base + rows, :] = do_ref[:, c : c + LANES]
        block = dot_terms[h * per_group : (h + 1) * per_group]
        block = jnp.concatenate([block, jnp.zeros((8 - per_group, LANES), F32)], axis=0)
        out_ref[h, 2 * per_group * rows :, :] = block.astype(BF16)


def relay_kernel(h_ref, lse_ref, out_ref):
    groups = h_ref.shape[0]
    per_group = lse_ref.shape[0] // groups
    rows = 32
    lse = lse_ref[...].astype(F32)
    quarters = groups // 2
    for g in range(per_group):
        for u in range(quarters):
            for a in range(2):
                r = (a * per_group + g) * quarters + u
                base = (a * per_group + g) * rows
                stats = []
                for part in range(2):
                    src = 2 * u + part
                    out_ref[r, part * rows : (part + 1) * rows, :] = h_ref[src, base : base + rows, :]
                    if a == 0:
                        stats.append(lse[g * groups + src : g * groups + src + 1])
                    else:
                        tile = h_ref[src, 2 * per_group * rows :, :].astype(F32)
                        stats.append(tile[g : g + 1])
                stats.append(jnp.zeros((6, LANES), F32))
                out_ref[r, 2 * rows :, :] = jnp.concatenate(stats, axis=0).astype(BF16)


def gather_kernel(src_ref, fill_ref, in_ref, out_hbm, out_ref, sems):
    owners = out_ref.shape[0]
    fill = fill_ref[0].astype(F32)
    count = 4

    def leave(part):
        at = pl.ds(part * count, count)
        return pltpu.make_async_copy(out_ref.at[at], out_hbm.at[at], sems.at[part])

    def body(part, carry):
        for k in range(count):
            j = part * count + k
            stats = []
            for slot in range(SLOTS):
                src = src_ref[j * SLOTS + slot]
                at = jnp.maximum(src, 0)
                out_ref[j, slot * 64 : (slot + 1) * 64, :] = in_ref[at, 0:64, :]
                tile = in_ref[at, 64:72, :].astype(F32)
                stats.append(jnp.where(src >= 0, tile[0:2], fill))
            stats.append(jnp.zeros((8 - 2 * SLOTS, LANES), F32))
            out_ref[j, SLOTS * 64 :, :] = jnp.concatenate(stats, axis=0).astype(BF16)
        leave(part).start()
        return carry

    lax.fori_loop(0, owners // count, body, 0)
    for part in range(owners // count):
        leave(part).wait()


def term_mask():
    row = lax.broadcasted_iota(jnp.int32, (32, LANES), 0)
    lane = lax.broadcasted_iota(jnp.int32, (32, LANES), 1)
    return (lane >= row * 4) & (lane < row * 4 + 4)


def assemble(x_ref, head, qx, dx):
    mask = term_mask()
    for a, out in ((0, qx), (1, dx)):
        for u in range(4):
            r = a * 16 + head * 4 + u
            stats = x_ref[r, SLOTS * 64 :, :].astype(F32)
            for slot in range(SLOTS):
                base = slot * 256 + u * 64
                out[base : base + 64, 0:LANES] = x_ref[r, slot * 64 : (slot + 1) * 64, :]
                for part in range(2):
                    row = slot * 2 + part
                    ext = jnp.where(mask, stats[row : row + 1], 0.0).astype(BF16)
                    out[base + part * 32 : base + part * 32 + 32, LANES:] = ext


def extend(block):
    return jnp.concatenate([block, jnp.full((block.shape[0], LANES), -1.0, BF16)], axis=1)


SCALE = LANES**-0.5
EXP_SCALE = SCALE * math.log2(math.e)


def query_kernel(x_ref, k_hbm, v_hbm, out_hbm, k_ref, v_ref, out_ref, qx, dx, sems, out_sems):
    per_group = k_ref.shape[0]

    def fetch(head, which):
        src, dst = ((k_hbm, k_ref), (v_hbm, v_ref))[which]
        at = pl.ds(pl.multiple_of(head * LANES, LANES), LANES)
        return pltpu.make_async_copy(src.at[:, at], dst.at[head], sems.at[head, which])

    def leave(head):
        at = pl.ds(head * 8, 8)
        return pltpu.make_async_copy(out_ref.at[at], out_hbm.at[at], out_sems.at[head])

    for head in range(per_group):
        fetch(head, 0).start()
        fetch(head, 1).start()

    def body(head, carry):
        assemble(x_ref, head, qx, dx)
        fetch(head, 0).wait()
        fetch(head, 1).wait()
        keys = k_ref[head]
        keys_ext = extend(keys)
        values_ext = extend(v_ref[head])
        for slot in range(SLOTS):
            at = slice(slot * 256, slot * 256 + 256)
            weights = jnp.exp2(dot(qx[at], keys_ext, NT) * EXP_SCALE)
            dscores = (weights * dot(dx[at], values_ext, NT)).astype(BF16)
            part = (dot(dscores, keys) * SCALE).astype(BF16)
            for e in range(8):
                out_ref[head * 8 + e, slot * 32 : (slot + 1) * 32, :] = part[e * 32 : (e + 1) * 32]
        leave(head).start()
        return carry

    lax.fori_loop(0, per_group, body, 0)
    for head in range(per_group):
        leave(head).wait()


def context_kernel(x_ref, k_ref, v_ref, dk_ref, dv_ref, qx, dx, *, chunk):
    head = pl.program_id(0)
    assemble(x_ref, head, qx, dx)

    def body(i, carry):
        at = pl.ds(pl.multiple_of(i * chunk, chunk), chunk)
        weights = jnp.exp2(dot(extend(k_ref[at, :]), qx[...], NT) * EXP_SCALE)
        dscores = (weights * dot(extend(v_ref[at, :]), dx[...], NT)).astype(BF16)
        dv_ref[at, :] = dot(weights.astype(BF16), dx[:, 0:LANES]).astype(BF16)
        dk_ref[at, :] = (dot(dscores, qx[:, 0:LANES]) * SCALE).astype(BF16)
        return carry

    lax.fori_loop(0, k_ref.shape[0] // chunk, body, 0, unroll=True)


def own_kernel(h_ref, kv_ref, lse_ref, dq_ref, dk_ref, dv_ref, qx, dx, kx, vx):
    head = pl.program_id(0)
    groups = h_ref.shape[0]
    mask = term_mask()
    lse = lse_ref[0].astype(F32)
    kx[:, LANES:] = jnp.full((kx.shape[0], LANES), -1.0, BF16)
    vx[:, LANES:] = jnp.full((kx.shape[0], LANES), -1.0, BF16)
    for src in range(groups):
        at = slice(src * 32, src * 32 + 32)
        first = pl.ds(pl.multiple_of(head * 32, 32), 32)
        second = pl.ds(pl.multiple_of(head * 32 + 128, 32), 32)
        qx[at, 0:LANES] = h_ref[src, first, :]
        dx[at, 0:LANES] = h_ref[src, second, :]
        kx[at, 0:LANES] = kv_ref[src, first, :]
        vx[at, 0:LANES] = kv_ref[src, second, :]
        qx[at, LANES:] = jnp.where(mask, lse[src : src + 1], 0.0).astype(BF16)
        tile = h_ref[src, 256:, :].astype(F32)
        at_head = lax.broadcasted_iota(jnp.int32, tile.shape, 0) == head
        row = jnp.sum(jnp.where(at_head, tile, 0.0), axis=0, keepdims=True)
        dx[at, LANES:] = jnp.where(mask, row, 0.0).astype(BF16)
    shape = (qx.shape[0], kx.shape[0])
    allowed = lax.broadcasted_iota(jnp.int32, shape, 0) >= lax.broadcasted_iota(jnp.int32, shape, 1)
    weights = jnp.where(allowed, jnp.exp2(dot(qx[...], kx[...], NT) * EXP_SCALE), 0.0)
    dscores = (weights * dot(dx[...], vx[...], NT)).astype(BF16)
    dq_ref[...] = dot(dscores, kx[:, 0:LANES]) * SCALE
    dk_ref[...] = (dot(dscores, qx[:, 0:LANES], TN) * SCALE).astype(BF16)
    dv_ref[...] = dot(weights.astype(BF16), dx[:, 0:LANES], TN).astype(BF16)


def pair_kernel(owner_ref, row_ref, in_ref, out_ref):
    def body(b, carry):
        total = None
        for s in range(2):
            row = pl.multiple_of(row_ref[b * 2 + s], 32)
            value = in_ref[owner_ref[b * 2 + s], pl.ds(row, 32), :].astype(F32)
            total = value if total is None else total + value
        out_ref[b] = total.astype(BF16)
        return carry

    lax.fori_loop(0, out_ref.shape[0], body, 0, unroll=4)


def finish_kernel(in_ref, own_ref, out_ref):
    count = in_ref.shape[0] // 4
    for g in range(4):
        part = in_ref[g * count : (g + 1) * count].astype(F32).reshape(own_ref.shape[0], LANES)
        at = slice(g * LANES, (g + 1) * LANES)
        out_ref[:, at] = (part + own_ref[:, at]).astype(BF16)


def per_device(queries, new_keys, new_values, attn_out, out_grad, logsumexp, ctx_keys, ctx_values, selected):
    owners = lax.axis_size("seq")
    groups = lax.axis_size("head")
    per_group, block_rows = logsumexp.shape
    rows = queries.shape[0]
    key_rows, features = ctx_keys.shape
    relay = lax.axis_index("seq")

    flat = selected.reshape(-1)
    order = jnp.arange(flat.shape[0])
    same = flat[:, None] == flat[None, :]
    slot_of = jnp.sum(same & (order[None, :] < order[:, None]), axis=1).astype(jnp.int32)
    place = flat * SLOTS + slot_of
    hit = place[None, :] == jnp.arange(owners * SLOTS)[:, None]
    source = jnp.max(jnp.where(hit, (order // selected.shape[1])[None, :], -1), axis=1).astype(jnp.int32)
    fill = jnp.where(relay < owners // 2, FILL, 0.0).astype(F32).reshape(1)

    hbm = pl.BlockSpec(memory_space=pltpu.HBM)
    head_out = pl.pallas_call(
        prepare_kernel,
        out_shape=jax.ShapeDtypeStruct((groups, 2 * per_group * rows + 8, LANES), BF16),
        in_specs=[hbm] * 3,
        out_specs=vmem(),
        scratch_shapes=[pltpu.VMEM(queries.shape, BF16)] * 3 + [pltpu.SemaphoreType.DMA((3,))],
        compiler_params=params(),
        name="prepare",
    )(in_hbm(queries), in_hbm(out_grad), in_hbm(attn_out))
    lse_terms = pl.pallas_call(
        lse_kernel,
        out_shape=jax.ShapeDtypeStruct((per_group * groups, LANES), BF16),
        in_specs=[vmem()],
        out_specs=vmem(),
        compiler_params=params(),
        name="lse_terms",
    )(logsumexp.reshape(per_group * groups, rows))
    window = lax.all_to_all(head_out, "head", split_axis=0, concat_axis=0, tiled=True)

    pieces = pl.pallas_call(
        relay_kernel,
        out_shape=jax.ShapeDtypeStruct((owners, 72, LANES), BF16),
        in_specs=[vmem()] * 2,
        out_specs=vmem(),
        compiler_params=params(),
        name="relay",
    )(window, lse_terms)
    held = lax.all_to_all(pieces, "seq", split_axis=0, concat_axis=0, tiled=True)

    smem = pl.BlockSpec(memory_space=pltpu.SMEM)
    outgoing = pl.pallas_call(
        gather_kernel,
        out_shape=jax.ShapeDtypeStruct((owners, SLOTS * 64 + 8, LANES), BF16),
        in_specs=[smem, smem, vmem()],
        out_specs=hbm,
        scratch_shapes=[pltpu.VMEM((owners, SLOTS * 64 + 8, LANES), BF16), pltpu.SemaphoreType.DMA((8,))],
        compiler_params=params(),
        name="gather",
    )(source, fill, held)
    items = lax.all_to_all(outgoing, "seq", split_axis=0, concat_axis=0, tiled=True)

    pair = [
        tensor.reshape(rows, groups, per_group, LANES).transpose(1, 2, 0, 3).reshape(groups, per_group * rows, LANES)
        for tensor in (new_keys, new_values)
    ]
    items, pair = lax.optimization_barrier((items, jnp.concatenate(pair, axis=1)))
    own_kv = lax.all_to_all(pair, "head", split_axis=0, concat_axis=0, tiled=True)

    slot_rows = SLOTS * block_rows
    work = 2 * slot_rows * key_rows * LANES * per_group
    ctx_keys, ctx_values = in_hbm(ctx_keys), in_hbm(ctx_values)
    wide = pltpu.VMEM((slot_rows, 2 * LANES), BF16)
    parts = pl.pallas_call(
        query_kernel,
        out_shape=jax.ShapeDtypeStruct((owners, SLOTS * 32, LANES), BF16),
        in_specs=[vmem(), hbm, hbm],
        out_specs=hbm,
        scratch_shapes=[pltpu.VMEM((per_group, key_rows, LANES), BF16)] * 2
        + [pltpu.VMEM((owners, SLOTS * 32, LANES), BF16), wide, wide]
        + [pltpu.SemaphoreType.DMA((per_group, 2)), pltpu.SemaphoreType.DMA((per_group,))],
        compiler_params=params(32),
        cost_estimate=pl.CostEstimate(flops=8 * work, bytes_accessed=6 << 20, transcendentals=0),
        name="query_parts",
    )(items, ctx_keys, ctx_values)

    parts, own_kv = lax.optimization_barrier((parts, own_kv))
    returned = lax.all_to_all(parts, "seq", split_axis=0, concat_axis=0, tiled=True)

    items_later, _ = lax.optimization_barrier((items, parts))
    context_spec = pl.BlockSpec((key_rows, LANES), lambda g: (0, g))
    items_spec = pl.BlockSpec((owners, SLOTS * 64 + 8, LANES), lambda g: (0, 0, 0))
    ctx_key_grad, ctx_value_grad = pl.pallas_call(
        functools.partial(context_kernel, chunk=256),
        grid=(per_group,),
        out_shape=(jax.ShapeDtypeStruct((key_rows, features), BF16),) * 2,
        in_specs=[items_spec, context_spec, context_spec],
        out_specs=(context_spec, context_spec),
        scratch_shapes=[wide, wide],
        compiler_params=params(24),
        cost_estimate=pl.CostEstimate(flops=10 * work, bytes_accessed=10 << 20, transcendentals=0),
        name="context_grads",
    )(items_later, ctx_keys, ctx_values)

    returned, ctx_key_grad, ctx_value_grad = lax.optimization_barrier((returned, ctx_key_grad, ctx_value_grad))
    summed = pl.pallas_call(
        pair_kernel,
        out_shape=jax.ShapeDtypeStruct((owners, 32, LANES), BF16),
        in_specs=[smem, smem, vmem()],
        out_specs=vmem(),
        compiler_params=params(),
        name="pair_sum",
    )(flat, slot_of * 32, returned)
    home = lax.all_to_all(summed, "seq", split_axis=0, concat_axis=0, tiled=True)
    own_kv, _ = lax.optimization_barrier((own_kv, summed))
    head_spec = pl.BlockSpec((block_rows, LANES), lambda g: (0, g))
    own_dq, new_key_grad, new_value_grad = pl.pallas_call(
        own_kernel,
        grid=(per_group,),
        out_shape=(
            jax.ShapeDtypeStruct((block_rows, features), F32),
            jax.ShapeDtypeStruct((block_rows, features), BF16),
            jax.ShapeDtypeStruct((block_rows, features), BF16),
        ),
        in_specs=[
            pl.BlockSpec(window.shape, lambda g: (0, 0, 0)),
            pl.BlockSpec(own_kv.shape, lambda g: (0, 0, 0)),
            pl.BlockSpec((1, groups, LANES), lambda g: (g, 0, 0)),
        ],
        out_specs=(head_spec, head_spec, head_spec),
        scratch_shapes=[pltpu.VMEM((block_rows, 2 * LANES), BF16)] * 4,
        compiler_params=params(),
        cost_estimate=pl.CostEstimate(flops=10 * block_rows * block_rows * features, bytes_accessed=2 << 20, transcendentals=0),
        name="own_set",
    )(window, own_kv, lse_terms.reshape(per_group, groups, LANES))

    query_grad = pl.pallas_call(
        finish_kernel,
        out_shape=jax.ShapeDtypeStruct((block_rows, features), BF16),
        in_specs=[vmem()] * 2,
        out_specs=vmem(),
        compiler_params=params(),
        name="finish",
    )(home, own_dq)
    return (query_grad, new_key_grad, new_value_grad, ctx_key_grad, ctx_value_grad)


def solution(mesh):
    in_specs = (
        P(("seq", "head"), None),
        P(("seq", "head"), None),
        P(("seq", "head"), None),
        P(("seq", "head"), None),
        P(("seq", "head"), None),
        P("head", "seq"),
        P("seq", "head"),
        P("seq", "head"),
        P(),
    )
    out_specs = (P("seq", "head"),) * 5
    return jax.shard_map(per_device, mesh=mesh, in_specs=in_specs, out_specs=out_specs, check_vma=False)
```

```python
import functools
import math

import jax
import jax.numpy as jnp
from jax import lax
from jax.experimental import pallas as pl
from jax.experimental.pallas import tpu as pltpu
from jax.sharding import PartitionSpec as P

BF16 = jnp.bfloat16
F32 = jnp.float32
LANES = 128
MIB = 1024 * 1024
SLOTS = 3
NT = (((1,), (1,)), ((), ()))
TN = (((0,), (0,)), ((), ()))
FILL = 1e5


def dot(lhs, rhs, dims=(((1,), (0,)), ((), ()))):
    return lax.dot_general(lhs, rhs, dims, preferred_element_type=F32)


def vmem():
    return pl.BlockSpec(memory_space=pltpu.VMEM)


def in_hbm(array):
    return pltpu.with_memory_space_constraint(array, pltpu.HBM)


def params(mib=8):
    return pltpu.CompilerParams(vmem_limit_bytes=mib * MIB)


def spread(values, term):
    high = values.astype(BF16)
    low = (values - high.astype(F32)).astype(BF16)
    shape = (values.shape[1], LANES)
    at = lax.broadcasted_iota(jnp.int32, shape, 0) * 4 + term
    lane = lax.broadcasted_iota(jnp.int32, shape, 1)
    out = dot(high, jnp.where(lane == at, 1.0, 0.0).astype(BF16))
    return out + dot(low, jnp.where(lane == at + 1, 1.0, 0.0).astype(BF16))


def statistics_kernel(lse_ref, dots_ref, out_ref):
    out_ref[...] = (spread(lse_ref[...] * math.sqrt(LANES), 0) + spread(dots_ref[...], 2)).astype(BF16)


def prepare_kernel(q_hbm, do_hbm, o_hbm, out_hbm, dots_ref, q_ref, do_ref, o_ref, out_ref, sems, out_sems):
    copies = [
        pltpu.make_async_copy(src, dst, sems.at[n])
        for n, (src, dst) in enumerate(((q_hbm, q_ref), (do_hbm, do_ref), (o_hbm, o_ref)))
    ]
    for copy in copies:
        copy.start()
    rows, features = q_ref.shape
    heads = features // LANES
    groups, _, _ = dots_ref.shape
    per_group = heads // groups
    octets = rows // 8
    leaving = []
    for a, ref in enumerate((q_ref, do_ref)):
        copies[a].wait()
        for g in range(per_group):
            for o in range(octets):
                for h in range(groups):
                    c = (h * per_group + g) * LANES
                    out_ref[((a * per_group + g) * octets + o) * groups + h] = ref[o * 8 : o * 8 + 8, c : c + LANES]
        half = pl.ds(a * per_group * octets * groups, per_group * octets * groups)
        leaving.append(pltpu.make_async_copy(out_ref.at[half], out_hbm.at[half], out_sems.at[a]))
        leaving[a].start()
    copies[2].wait()
    product = do_ref[...].astype(F32) * o_ref[...].astype(F32)
    high = product.astype(BF16)
    low = (product - high.astype(F32)).astype(BF16)
    head_at = lax.broadcasted_iota(jnp.int32, (heads, features), 0)
    lane = lax.broadcasted_iota(jnp.int32, (heads, features), 1)
    pick = jnp.where((lane >= head_at * LANES) & (lane < head_at * LANES + LANES), 1.0, 0.0).astype(BF16)
    dots = dot(pick, high, NT) + dot(pick, low, NT)
    for h in range(groups):
        dots_ref[h] = dots[h * per_group : (h + 1) * per_group]
    for copy in leaving:
        copy.wait()


def gather_kernel(src_ref, in_ref, stats_ref, out_hbm, out_ref, sems):
    owners = out_ref.shape[0]
    count = 4

    def leave(part):
        at = pl.ds(part * count, count)
        return pltpu.make_async_copy(out_ref.at[at], out_hbm.at[at], sems.at[part])

    def body(part, carry):
        stats = stats_ref[...]
        for k in range(count):
            j = part * count + k
            for slot in range(SLOTS):
                at = jnp.maximum(src_ref[j * SLOTS + slot], 0)
                out_ref[j, slot * 64 : (slot + 1) * 64, :] = in_ref[at]
            out_ref[j, SLOTS * 64 :, :] = stats
        leave(part).start()
        return carry

    lax.fori_loop(0, owners // count, body, 0)
    for part in range(owners // count):
        leave(part).wait()


def load_statistics(src_ref, x_ref, stats_ref):
    lane = lax.broadcasted_iota(jnp.int32, (32, LANES), 1)
    is_lse = lane % 4 < 2
    for slot in range(SLOTS):
        src = src_ref[slot]
        tile = x_ref[jnp.maximum(src, 0), SLOTS * 64 :, :].astype(F32)
        stats_ref[slot] = jnp.where(is_lse & (src < 0), FILL, tile)


def assemble(x_ref, stats_ref, head, qx, dx):
    row = lax.broadcasted_iota(jnp.int32, (32, LANES), 0)
    lane = lax.broadcasted_iota(jnp.int32, (32, LANES), 1)
    for slot in range(SLOTS):
        stats = stats_ref[slot, pl.ds(pl.multiple_of(head * 8, 8), 8), :]
        for a, out in ((0, qx), (1, dx)):
            first = row * 4 + 2 * a
            mask = (lane == first) | (lane == first + 1)
            for u in range(4):
                base = slot * 256 + u * 64
                out[base : base + 64, 0:LANES] = x_ref[a * 16 + head * 4 + u, slot * 64 : (slot + 1) * 64, :]
            for e in range(8):
                base = slot * 256 + e * 32
                out[base : base + 32, LANES:] = jnp.where(mask, stats[e : e + 1], 0.0).astype(BF16)


def extend(block):
    return jnp.concatenate([block, jnp.full((block.shape[0], LANES), -1.0, BF16)], axis=1)


SCALE = LANES**-0.5
EXP_SCALE = SCALE * math.log2(math.e)


def query_kernel(src_ref, x_ref, k_hbm, v_hbm, out_hbm, k_ref, v_ref, out_ref, qx, dx, stats, sems, out_sems):
    per_group = k_ref.shape[0]

    def fetch(head, which):
        src, dst = ((k_hbm, k_ref), (v_hbm, v_ref))[which]
        at = pl.ds(pl.multiple_of(head * LANES, LANES), LANES)
        return pltpu.make_async_copy(src.at[:, at], dst.at[head], sems.at[head, which])

    def leave(head):
        at = pl.ds(head * 8, 8)
        return pltpu.make_async_copy(out_ref.at[at], out_hbm.at[at], out_sems.at[head])

    for head in range(per_group):
        fetch(head, 0).start()
        fetch(head, 1).start()
    load_statistics(src_ref, x_ref, stats)

    def body(head, carry):
        assemble(x_ref, stats, head, qx, dx)
        fetch(head, 0).wait()
        fetch(head, 1).wait()
        keys = k_ref[head]
        keys_ext = extend(keys)
        values_ext = extend(v_ref[head])
        for slot in range(SLOTS):
            at = slice(slot * 256, slot * 256 + 256)
            weights = jnp.exp2(dot(qx[at], keys_ext, NT) * EXP_SCALE)
            dscores = (weights * dot(dx[at], values_ext, NT)).astype(BF16)
            part = (dot(dscores, keys) * SCALE).astype(BF16)
            for e in range(8):
                out_ref[head * 8 + e, slot * 32 : (slot + 1) * 32, :] = part[e * 32 : (e + 1) * 32]
        leave(head).start()
        return carry

    lax.fori_loop(0, per_group, body, 0)
    for head in range(per_group):
        leave(head).wait()


def context_kernel(src_ref, x_ref, k_ref, v_ref, dk_ref, dv_ref, qx, dx, stats, *, chunk):
    load_statistics(src_ref, x_ref, stats)
    assemble(x_ref, stats, pl.program_id(0), qx, dx)

    def body(i, carry):
        at = pl.ds(pl.multiple_of(i * chunk, chunk), chunk)
        weights = jnp.exp2(dot(extend(k_ref[at, :]), qx[...], NT) * EXP_SCALE)
        dscores = (weights * dot(extend(v_ref[at, :]), dx[...], NT)).astype(BF16)
        dv_ref[at, :] = dot(weights.astype(BF16), dx[:, 0:LANES]).astype(BF16)
        dk_ref[at, :] = (dot(dscores, qx[:, 0:LANES]) * SCALE).astype(BF16)
        return carry

    lax.fori_loop(0, k_ref.shape[0] // chunk, body, 0, unroll=True)


def own_kernel(me_ref, w_ref, stats_ref, dq_ref, dk_ref, dv_ref, qx, dx, kx, vx):
    head = pl.program_id(0)
    groups = w_ref.shape[0]
    row = lax.broadcasted_iota(jnp.int32, (8, LANES), 0)
    lane = lax.broadcasted_iota(jnp.int32, (8, LANES), 1)
    stats = stats_ref[0].astype(F32)
    kx[:, LANES:] = jnp.full((kx.shape[0], LANES), -1.0, BF16)
    vx[:, LANES:] = jnp.full((kx.shape[0], LANES), -1.0, BF16)
    for src in range(groups):
        at = slice(src * 32, src * 32 + 32)
        for n, ref in enumerate((qx, dx, kx, vx)):
            piece = pl.ds(pl.multiple_of(n * 128 + head * 32, 32), 32)
            ref[at, 0:LANES] = w_ref[me_ref[0] ^ src, piece, :]
        for a, ref in ((0, qx), (1, dx)):
            first = ((src % 4) * 8 + row) * 4 + 2 * a
            mask = (lane == first) | (lane == first + 1)
            e = src // 4
            terms = [jnp.where(mask, stats[o * 2 + e : o * 2 + e + 1], 0.0) for o in range(4)]
            ref[at, LANES:] = jnp.concatenate(terms, axis=0).astype(BF16)
    shape = (qx.shape[0], kx.shape[0])
    allowed = lax.broadcasted_iota(jnp.int32, shape, 0) >= lax.broadcasted_iota(jnp.int32, shape, 1)
    weights = jnp.where(allowed, jnp.exp2(dot(qx[...], kx[...], NT) * EXP_SCALE), 0.0)
    dscores = (weights * dot(dx[...], vx[...], NT)).astype(BF16)
    dq_ref[...] = dot(dscores, kx[:, 0:LANES]) * SCALE
    dk_ref[...] = (dot(dscores, qx[:, 0:LANES], TN) * SCALE).astype(BF16)
    dv_ref[...] = dot(weights.astype(BF16), dx[:, 0:LANES], TN).astype(BF16)


def pair_kernel(owner_ref, row_ref, in_ref, out_ref):
    def body(b, carry):
        total = None
        for s in range(2):
            row = pl.multiple_of(row_ref[b * 2 + s], 32)
            value = in_ref[owner_ref[b * 2 + s], pl.ds(row, 32), :].astype(F32)
            total = value if total is None else total + value
        out_ref[b] = total.astype(BF16)
        return carry

    lax.fori_loop(0, out_ref.shape[0], body, 0, unroll=4)


def finish_kernel(in_ref, own_ref, out_ref):
    for g in range(4):
        at = slice(g * LANES, (g + 1) * LANES)
        parts = [in_ref[g * 8 + e].astype(F32) for e in range(8)]
        for h in range(8):
            octet = slice((h % 4) * 8, (h % 4) * 8 + 8)
            block = jnp.concatenate([parts[o * 2 + h // 4][octet] for o in range(4)], axis=0)
            rows = slice(h * 32, h * 32 + 32)
            out_ref[rows, at] = (block + own_ref[rows, at]).astype(BF16)


def per_device(queries, new_keys, new_values, attn_out, out_grad, logsumexp, ctx_keys, ctx_values, selected):
    owners = lax.axis_size("seq")
    groups = lax.axis_size("head")
    per_group, block_rows = logsumexp.shape
    rows = queries.shape[0]
    key_rows, features = ctx_keys.shape
    relay = lax.axis_index("seq")

    flat = selected.reshape(-1)
    order = jnp.arange(flat.shape[0])
    same = flat[:, None] == flat[None, :]
    slot_of = jnp.sum(same & (order[None, :] < order[:, None]), axis=1).astype(jnp.int32)
    place = flat * SLOTS + slot_of
    hit = place[None, :] == jnp.arange(owners * SLOTS)[:, None]
    source = jnp.max(jnp.where(hit, (order // selected.shape[1])[None, :], -1), axis=1).astype(jnp.int32)
    mine = lax.dynamic_slice(source, (relay * SLOTS,), (SLOTS,))
    me = lax.axis_index("head").astype(jnp.int32)

    def swap(tensor):
        parts = [lax.dynamic_index_in_dim(tensor, me, 0, keepdims=False)]
        for k in range(1, groups):
            part = lax.dynamic_index_in_dim(tensor, me ^ k, 0, keepdims=False)
            parts.append(lax.ppermute(part, "head", [(i, i ^ k) for i in range(groups)]))
        return parts

    hbm = pl.BlockSpec(memory_space=pltpu.HBM)
    smem = pl.BlockSpec(memory_space=pltpu.SMEM)
    tiles = owners * groups
    pieces, dots = pl.pallas_call(
        prepare_kernel,
        out_shape=(
            jax.ShapeDtypeStruct((tiles, 8, LANES), BF16),
            jax.ShapeDtypeStruct((groups, per_group, rows), F32),
        ),
        in_specs=[hbm] * 3,
        out_specs=(hbm, vmem()),
        scratch_shapes=[pltpu.VMEM(queries.shape, BF16)] * 3
        + [pltpu.VMEM((tiles, 8, LANES), BF16), pltpu.SemaphoreType.DMA((3,)), pltpu.SemaphoreType.DMA((2,))],
        compiler_params=params(),
        name="prepare",
    )(in_hbm(queries), in_hbm(out_grad), in_hbm(attn_out))
    held = lax.all_to_all(pieces, ("seq", "head"), split_axis=0, concat_axis=0, tiled=True)
    held = held.reshape(owners, 64, LANES)

    dots = jnp.take(jnp.stack(swap(dots)), me ^ jnp.arange(groups), axis=0)
    dots = dots.reshape(2, 4, per_group, 4, 8).transpose(2, 3, 0, 1, 4).reshape(32, 32)
    lse = logsumexp.reshape(per_group, 2, 4, 4, 8).transpose(0, 3, 1, 2, 4).reshape(32, 32)
    stats = pl.pallas_call(
        statistics_kernel,
        out_shape=jax.ShapeDtypeStruct((32, LANES), BF16),
        in_specs=[vmem()] * 2,
        out_specs=vmem(),
        compiler_params=params(),
        name="statistics",
    )(lse, dots)

    item_rows = SLOTS * 64 + 32
    outgoing = pl.pallas_call(
        gather_kernel,
        out_shape=jax.ShapeDtypeStruct((owners, item_rows, LANES), BF16),
        in_specs=[smem, vmem(), vmem()],
        out_specs=hbm,
        scratch_shapes=[pltpu.VMEM((owners, item_rows, LANES), BF16), pltpu.SemaphoreType.DMA((8,))],
        compiler_params=params(),
        name="gather",
    )(source, held, stats)

    window = [
        tensor.reshape(rows, groups, per_group, LANES).transpose(1, 2, 0, 3).reshape(groups, per_group * rows, LANES)
        for tensor in (queries, out_grad, new_keys, new_values)
    ]
    outgoing, window = lax.optimization_barrier((outgoing, jnp.concatenate(window, axis=1)))
    items = lax.all_to_all(outgoing, "seq", split_axis=0, concat_axis=0, tiled=True)
    window = swap(window)

    slot_rows = SLOTS * block_rows
    work = 2 * slot_rows * key_rows * LANES * per_group
    ctx_keys, ctx_values = in_hbm(ctx_keys), in_hbm(ctx_values)
    wide = pltpu.VMEM((slot_rows, 2 * LANES), BF16)
    slot_stats = pltpu.VMEM((SLOTS, 32, LANES), F32)
    parts = pl.pallas_call(
        query_kernel,
        out_shape=jax.ShapeDtypeStruct((owners, SLOTS * 32, LANES), BF16),
        in_specs=[smem, vmem(), hbm, hbm],
        out_specs=hbm,
        scratch_shapes=[pltpu.VMEM((per_group, key_rows, LANES), BF16)] * 2
        + [pltpu.VMEM((owners, SLOTS * 32, LANES), BF16), wide, wide, slot_stats]
        + [pltpu.SemaphoreType.DMA((per_group, 2)), pltpu.SemaphoreType.DMA((per_group,))],
        compiler_params=params(32),
        cost_estimate=pl.CostEstimate(flops=8 * work, bytes_accessed=6 << 20, transcendentals=0),
        name="query_parts",
    )(mine, items, ctx_keys, ctx_values)

    returned = lax.all_to_all(parts, "seq", split_axis=0, concat_axis=0, tiled=True)

    items_later, _ = lax.optimization_barrier((items, parts))
    context_spec = pl.BlockSpec((key_rows, LANES), lambda g: (0, g))
    items_spec = pl.BlockSpec((owners, item_rows, LANES), lambda g: (0, 0, 0))
    ctx_key_grad, ctx_value_grad = pl.pallas_call(
        functools.partial(context_kernel, chunk=256),
        grid=(per_group,),
        out_shape=(jax.ShapeDtypeStruct((key_rows, features), BF16),) * 2,
        in_specs=[smem, items_spec, context_spec, context_spec],
        out_specs=(context_spec, context_spec),
        scratch_shapes=[wide, wide, slot_stats],
        compiler_params=params(24),
        cost_estimate=pl.CostEstimate(flops=10 * work, bytes_accessed=10 << 20, transcendentals=0),
        name="context_grads",
    )(mine, items_later, ctx_keys, ctx_values)

    returned, ctx_key_grad, ctx_value_grad = lax.optimization_barrier((returned, ctx_key_grad, ctx_value_grad))
    summed = pl.pallas_call(
        pair_kernel,
        out_shape=jax.ShapeDtypeStruct((owners, 32, LANES), BF16),
        in_specs=[smem, smem, vmem()],
        out_specs=vmem(),
        compiler_params=params(),
        name="pair_sum",
    )(flat, slot_of * 32, returned)
    home = lax.all_to_all(summed, "seq", split_axis=0, concat_axis=0, tiled=True)
    window, _ = lax.optimization_barrier((jnp.stack(window), summed))
    head_spec = pl.BlockSpec((block_rows, LANES), lambda g: (0, g))
    own_dq, new_key_grad, new_value_grad = pl.pallas_call(
        own_kernel,
        grid=(per_group,),
        out_shape=(
            jax.ShapeDtypeStruct((block_rows, features), F32),
            jax.ShapeDtypeStruct((block_rows, features), BF16),
            jax.ShapeDtypeStruct((block_rows, features), BF16),
        ),
        in_specs=[
            smem,
            pl.BlockSpec(window.shape, lambda g: (0, 0, 0)),
            pl.BlockSpec((1, groups, LANES), lambda g: (g, 0, 0)),
        ],
        out_specs=(head_spec, head_spec, head_spec),
        scratch_shapes=[pltpu.VMEM((block_rows, 2 * LANES), BF16)] * 4,
        compiler_params=params(),
        cost_estimate=pl.CostEstimate(flops=10 * block_rows * block_rows * features, bytes_accessed=2 << 20, transcendentals=0),
        name="own_set",
    )(me.reshape(1), window, stats.reshape(per_group, groups, LANES))

    query_grad = pl.pallas_call(
        finish_kernel,
        out_shape=jax.ShapeDtypeStruct((block_rows, features), BF16),
        in_specs=[vmem()] * 2,
        out_specs=vmem(),
        compiler_params=params(),
        name="finish",
    )(home, own_dq)
    return (query_grad, new_key_grad, new_value_grad, ctx_key_grad, ctx_value_grad)


def solution(mesh):
    in_specs = (
        P(("seq", "head"), None),
        P(("seq", "head"), None),
        P(("seq", "head"), None),
        P(("seq", "head"), None),
        P(("seq", "head"), None),
        P("head", "seq"),
        P("seq", "head"),
        P("seq", "head"),
        P(),
    )
    out_specs = (P("seq", "head"),) * 5
    return jax.shard_map(per_device, mesh=mesh, in_specs=in_specs, out_specs=out_specs, check_vma=False)
```

```python
import functools
import math

import jax
import jax.numpy as jnp
from jax import lax
from jax.experimental import pallas as pl
from jax.experimental.pallas import tpu as pltpu
from jax.sharding import PartitionSpec as P

BF16 = jnp.bfloat16
F32 = jnp.float32
LANES = 128
MIB = 1024 * 1024
SLOTS = 3
NT = (((1,), (1,)), ((), ()))
TN = (((0,), (0,)), ((), ()))
FILL = 1e5


def dot(lhs, rhs, dims=(((1,), (0,)), ((), ()))):
    return lax.dot_general(lhs, rhs, dims, preferred_element_type=F32)


def vmem():
    return pl.BlockSpec(memory_space=pltpu.VMEM)


def in_hbm(array):
    return pltpu.with_memory_space_constraint(array, pltpu.HBM)


def params(mib=8):
    return pltpu.CompilerParams(vmem_limit_bytes=mib * MIB)


def spread(values, term):
    high = values.astype(BF16)
    low = (values - high.astype(F32)).astype(BF16)
    shape = (values.shape[1], LANES)
    at = lax.broadcasted_iota(jnp.int32, shape, 0) * 4 + term
    lane = lax.broadcasted_iota(jnp.int32, shape, 1)
    out = dot(high, jnp.where(lane == at, 1.0, 0.0).astype(BF16))
    return out + dot(low, jnp.where(lane == at + 1, 1.0, 0.0).astype(BF16))


def statistics_kernel(lse_ref, dots_ref, out_ref):
    out_ref[...] = (spread(lse_ref[...] * math.sqrt(LANES), 0) + spread(dots_ref[...], 2)).astype(BF16)


def prepare_kernel(q_hbm, do_hbm, out_hbm, q_ref, do_ref, out_ref, sems, out_sems, *, per_group):
    copies = [
        pltpu.make_async_copy(src, dst, sems.at[n]) for n, (src, dst) in enumerate(((q_hbm, q_ref), (do_hbm, do_ref)))
    ]
    for copy in copies:
        copy.start()
    rows, features = q_ref.shape
    octets = rows // 8
    heads = features // LANES
    groups = heads // per_group
    leaving = []
    for a, ref in enumerate((q_ref, do_ref)):
        copies[a].wait()
        for g in range(per_group):
            for o in range(octets):
                for h in range(groups):
                    c = (h * per_group + g) * LANES
                    out_ref[((a * per_group + g) * octets + o) * groups + h] = ref[o * 8 : o * 8 + 8, c : c + LANES]
        half = pl.ds(a * per_group * octets * groups, per_group * octets * groups)
        leaving.append(pltpu.make_async_copy(out_ref.at[half], out_hbm.at[half], out_sems.at[a]))
        leaving[a].start()
    for copy in leaving:
        copy.wait()


def dots_kernel(do_ref, o_ref, dots_ref):
    features = do_ref.shape[1]
    heads = features // LANES
    groups, per_group, _ = dots_ref.shape
    product = do_ref[...].astype(F32) * o_ref[...].astype(F32)
    high = product.astype(BF16)
    low = (product - high.astype(F32)).astype(BF16)
    head_at = lax.broadcasted_iota(jnp.int32, (heads, features), 0)
    lane = lax.broadcasted_iota(jnp.int32, (heads, features), 1)
    pick = jnp.where((lane >= head_at * LANES) & (lane < head_at * LANES + LANES), 1.0, 0.0).astype(BF16)
    dots = dot(pick, high, NT) + dot(pick, low, NT)
    for h in range(groups):
        dots_ref[h] = dots[h * per_group : (h + 1) * per_group]


def gather_kernel(src_ref, in_ref, stats_ref, out_hbm, out_ref, sems):
    owners = out_ref.shape[0]
    count = 4

    def leave(part):
        at = pl.ds(part * count, count)
        return pltpu.make_async_copy(out_ref.at[at], out_hbm.at[at], sems.at[part])

    def body(part, carry):
        stats = stats_ref[...]
        for k in range(count):
            j = part * count + k
            for slot in range(SLOTS):
                at = jnp.maximum(src_ref[j * SLOTS + slot], 0)
                out_ref[j, slot * 64 : (slot + 1) * 64, :] = in_ref[at]
            out_ref[j, SLOTS * 64 :, :] = stats
        leave(part).start()
        return carry

    lax.fori_loop(0, owners // count, body, 0)
    for part in range(owners // count):
        leave(part).wait()


def load_statistics(src_ref, x_ref, stats_ref):
    lane = lax.broadcasted_iota(jnp.int32, (32, LANES), 1)
    is_lse = lane % 4 < 2
    for slot in range(SLOTS):
        src = src_ref[slot]
        tile = x_ref[jnp.maximum(src, 0), SLOTS * 64 :, :].astype(F32)
        stats_ref[slot] = jnp.where(is_lse & (src < 0), FILL, tile)


def assemble(x_ref, stats_ref, head, qx, dx):
    row = lax.broadcasted_iota(jnp.int32, (32, LANES), 0)
    lane = lax.broadcasted_iota(jnp.int32, (32, LANES), 1)
    for slot in range(SLOTS):
        stats = stats_ref[slot, pl.ds(pl.multiple_of(head * 8, 8), 8), :]
        for a, out in ((0, qx), (1, dx)):
            first = row * 4 + 2 * a
            mask = (lane == first) | (lane == first + 1)
            for u in range(4):
                base = slot * 256 + u * 64
                out[base : base + 64, 0:LANES] = x_ref[a * 16 + head * 4 + u, slot * 64 : (slot + 1) * 64, :]
            for e in range(8):
                base = slot * 256 + e * 32
                out[base : base + 32, LANES:] = jnp.where(mask, stats[e : e + 1], 0.0).astype(BF16)


def extend(block):
    return jnp.concatenate([block, jnp.full((block.shape[0], LANES), -1.0, BF16)], axis=1)


SCALE = LANES**-0.5
EXP_SCALE = SCALE * math.log2(math.e)


def query_kernel(src_ref, x_ref, k_hbm, v_hbm, out_hbm, k_ref, v_ref, out_ref, qx, dx, stats, sems, out_sems):
    per_group = k_ref.shape[0]

    def fetch(head, which):
        src, dst = ((k_hbm, k_ref), (v_hbm, v_ref))[which]
        at = pl.ds(pl.multiple_of(head * LANES, LANES), LANES)
        return pltpu.make_async_copy(src.at[:, at], dst.at[head], sems.at[head, which])

    def leave(head):
        at = pl.ds(head * 8, 8)
        return pltpu.make_async_copy(out_ref.at[at], out_hbm.at[at], out_sems.at[head])

    fetch(0, 0).start()
    fetch(0, 1).start()
    load_statistics(src_ref, x_ref, stats)

    def body(head, carry):
        assemble(x_ref, stats, head, qx, dx)
        fetch(head, 0).wait()
        fetch(head, 1).wait()

        @pl.when(head + 1 < per_group)
        def _():
            fetch(head + 1, 0).start()
            fetch(head + 1, 1).start()

        keys = k_ref[head]
        keys_ext = extend(keys)
        values_ext = extend(v_ref[head])
        for slot in range(SLOTS):
            at = slice(slot * 256, slot * 256 + 256)
            weights = jnp.exp2(dot(qx[at], keys_ext, NT) * EXP_SCALE)
            dscores = (weights * dot(dx[at], values_ext, NT)).astype(BF16)
            part = (dot(dscores, keys) * SCALE).astype(BF16)
            for e in range(8):
                out_ref[head * 8 + e, slot * 32 : (slot + 1) * 32, :] = part[e * 32 : (e + 1) * 32]
        leave(head).start()
        return carry

    lax.fori_loop(0, per_group, body, 0)
    for head in range(per_group):
        leave(head).wait()


def context_kernel(src_ref, x_ref, k_ref, v_ref, *refs, chunk, first):
    dk_ref, dv_ref, qx, dx, stats = refs[-5:]
    load_statistics(src_ref, x_ref, stats)
    assemble(x_ref, stats, pl.program_id(0) + first, qx, dx)

    def body(i, carry):
        at = pl.ds(pl.multiple_of(i * chunk, chunk), chunk)
        weights = jnp.exp2(dot(extend(k_ref[at, :]), qx[...], NT) * EXP_SCALE)
        dscores = (weights * dot(extend(v_ref[at, :]), dx[...], NT)).astype(BF16)
        dv_ref[at, :] = dot(weights.astype(BF16), dx[:, 0:LANES]).astype(BF16)
        dk_ref[at, :] = (dot(dscores, qx[:, 0:LANES]) * SCALE).astype(BF16)
        return carry

    lax.fori_loop(0, k_ref.shape[0] // chunk, body, 0, unroll=True)


def own_kernel(me_ref, stats_ref, *refs):
    head = pl.program_id(0)
    window, (dq_ref, dk_ref, dv_ref, qx, dx, kx, vx) = refs[:-7], refs[-7:]
    row = lax.broadcasted_iota(jnp.int32, (8, LANES), 0)
    lane = lax.broadcasted_iota(jnp.int32, (8, LANES), 1)
    stats = stats_ref[0].astype(F32)
    kx[:, LANES:] = jnp.full((kx.shape[0], LANES), -1.0, BF16)
    vx[:, LANES:] = jnp.full((kx.shape[0], LANES), -1.0, BF16)
    for src, w_ref in enumerate(window):
        at = pl.ds(pl.multiple_of((me_ref[0] ^ src) * 32, 32), 32)
        for n, ref in enumerate((qx, dx, kx, vx)):
            piece = pl.ds(pl.multiple_of(n * 128 + head * 32, 32), 32)
            ref[at, 0:LANES] = w_ref[piece, :]
        at = slice(src * 32, src * 32 + 32)
        for a, ref in ((0, qx), (1, dx)):
            first = ((src % 4) * 8 + row) * 4 + 2 * a
            mask = (lane == first) | (lane == first + 1)
            e = src // 4
            terms = [jnp.where(mask, stats[o * 2 + e : o * 2 + e + 1], 0.0) for o in range(4)]
            ref[at, LANES:] = jnp.concatenate(terms, axis=0).astype(BF16)
    shape = (qx.shape[0], kx.shape[0])
    allowed = lax.broadcasted_iota(jnp.int32, shape, 0) >= lax.broadcasted_iota(jnp.int32, shape, 1)
    weights = jnp.where(allowed, jnp.exp2(dot(qx[...], kx[...], NT) * EXP_SCALE), 0.0)
    dscores = (weights * dot(dx[...], vx[...], NT)).astype(BF16)
    dq_ref[...] = dot(dscores, kx[:, 0:LANES]) * SCALE
    dk_ref[...] = (dot(dscores, qx[:, 0:LANES], TN) * SCALE).astype(BF16)
    dv_ref[...] = dot(weights.astype(BF16), dx[:, 0:LANES], TN).astype(BF16)


def pair_kernel(owner_ref, row_ref, in_ref, out_hbm, out_ref, sems):
    count = 8

    def leave(part):
        at = pl.ds(part * count, count)
        return pltpu.make_async_copy(out_ref.at[at], out_hbm.at[at], sems.at[part])

    def body(part, carry):
        for k in range(count):
            b = part * count + k
            total = None
            for s in range(2):
                row = pl.multiple_of(row_ref[b * 2 + s], 32)
                value = in_ref[owner_ref[b * 2 + s], pl.ds(row, 32), :].astype(F32)
                total = value if total is None else total + value
            out_ref[b] = total.astype(BF16)
        leave(part).start()
        return carry

    parts = out_ref.shape[0] // count
    lax.fori_loop(0, parts, body, 0)
    for part in range(parts):
        leave(part).wait()


def finish_kernel(in_ref, own_ref, out_ref):
    for g in range(4):
        at = slice(g * LANES, (g + 1) * LANES)
        parts = [in_ref[g * 8 + e].astype(F32) for e in range(8)]
        for h in range(8):
            octet = slice((h % 4) * 8, (h % 4) * 8 + 8)
            block = jnp.concatenate([parts[o * 2 + h // 4][octet] for o in range(4)], axis=0)
            rows = slice(h * 32, h * 32 + 32)
            out_ref[rows, at] = (block + own_ref[rows, at]).astype(BF16)


def per_device(queries, new_keys, new_values, attn_out, out_grad, logsumexp, ctx_keys, ctx_values, selected):
    owners = lax.axis_size("seq")
    groups = lax.axis_size("head")
    per_group, block_rows = logsumexp.shape
    rows = queries.shape[0]
    key_rows, features = ctx_keys.shape
    relay = lax.axis_index("seq")

    flat = selected.reshape(-1)
    order = jnp.arange(flat.shape[0])
    same = flat[:, None] == flat[None, :]
    slot_of = jnp.sum(same & (order[None, :] < order[:, None]), axis=1).astype(jnp.int32)
    place = flat * SLOTS + slot_of
    hit = place[None, :] == jnp.arange(owners * SLOTS)[:, None]
    source = jnp.max(jnp.where(hit, (order // selected.shape[1])[None, :], -1), axis=1).astype(jnp.int32)
    mine = lax.dynamic_slice(source, (relay * SLOTS,), (SLOTS,))
    me = lax.axis_index("head").astype(jnp.int32)

    def swap(tensor):
        parts = [lax.dynamic_index_in_dim(tensor, me, 0, keepdims=False)]
        for k in range(1, groups):
            part = lax.dynamic_index_in_dim(tensor, me ^ k, 0, keepdims=False)
            parts.append(lax.ppermute(part, "head", [(i, i ^ k) for i in range(groups)]))
        return parts

    hbm = pl.BlockSpec(memory_space=pltpu.HBM)
    smem = pl.BlockSpec(memory_space=pltpu.SMEM)
    tiles = owners * groups
    pieces = pl.pallas_call(
        functools.partial(prepare_kernel, per_group=per_group),
        out_shape=jax.ShapeDtypeStruct((tiles, 8, LANES), BF16),
        in_specs=[hbm] * 2,
        out_specs=hbm,
        scratch_shapes=[pltpu.VMEM(queries.shape, BF16)] * 2
        + [pltpu.VMEM((tiles, 8, LANES), BF16), pltpu.SemaphoreType.DMA((2,)), pltpu.SemaphoreType.DMA((2,))],
        compiler_params=params(),
        name="prepare",
    )(in_hbm(queries), in_hbm(out_grad))
    dots = pl.pallas_call(
        dots_kernel,
        out_shape=jax.ShapeDtypeStruct((groups, per_group, rows), F32),
        in_specs=[vmem()] * 2,
        out_specs=vmem(),
        compiler_params=params(),
        name="out_dot",
    )(*lax.optimization_barrier((out_grad, attn_out, pieces))[:2])
    held = lax.all_to_all(pieces, ("seq", "head"), split_axis=0, concat_axis=0, tiled=True)
    held = held.reshape(owners, 64, LANES)

    dots = jnp.take(jnp.stack(swap(dots)), me ^ jnp.arange(groups), axis=0)
    dots = dots.reshape(2, 4, per_group, 4, 8).transpose(2, 3, 0, 1, 4).reshape(32, 32)
    lse = logsumexp.reshape(per_group, 2, 4, 4, 8).transpose(0, 3, 1, 2, 4).reshape(32, 32)
    stats = pl.pallas_call(
        statistics_kernel,
        out_shape=jax.ShapeDtypeStruct((32, LANES), BF16),
        in_specs=[vmem()] * 2,
        out_specs=vmem(),
        compiler_params=params(),
        name="statistics",
    )(lse, dots)

    item_rows = SLOTS * 64 + 32
    outgoing = pl.pallas_call(
        gather_kernel,
        out_shape=jax.ShapeDtypeStruct((owners, item_rows, LANES), BF16),
        in_specs=[smem, vmem(), vmem()],
        out_specs=hbm,
        scratch_shapes=[pltpu.VMEM((owners, item_rows, LANES), BF16), pltpu.SemaphoreType.DMA((8,))],
        compiler_params=params(),
        name="gather",
    )(source, held, stats)

    window = [
        tensor.reshape(rows, groups, per_group, LANES).transpose(1, 2, 0, 3).reshape(groups, per_group * rows, LANES)
        for tensor in (queries, out_grad, new_keys, new_values)
    ]
    outgoing, window = lax.optimization_barrier((outgoing, jnp.concatenate(window, axis=1)))
    items = lax.all_to_all(outgoing, "seq", split_axis=0, concat_axis=0, tiled=True)
    window = swap(window)

    head_spec = pl.BlockSpec((block_rows, LANES), lambda g: (0, g))
    own_dq, new_key_grad, new_value_grad = pl.pallas_call(
        own_kernel,
        grid=(per_group,),
        out_shape=(
            jax.ShapeDtypeStruct((block_rows, features), F32),
            jax.ShapeDtypeStruct((block_rows, features), BF16),
            jax.ShapeDtypeStruct((block_rows, features), BF16),
        ),
        in_specs=[smem, pl.BlockSpec((1, groups, LANES), lambda g: (g, 0, 0))]
        + [pl.BlockSpec(piece.shape, lambda g: (0, 0)) for piece in window],
        out_specs=(head_spec, head_spec, head_spec),
        scratch_shapes=[pltpu.VMEM((block_rows, 2 * LANES), BF16)] * 4,
        compiler_params=params(),
        cost_estimate=pl.CostEstimate(flops=10 * block_rows * block_rows * features, bytes_accessed=2 << 20, transcendentals=0),
        name="own_set",
    )(me.reshape(1), stats.reshape(per_group, groups, LANES), *window)

    items, own_dq, new_key_grad, new_value_grad = lax.optimization_barrier((items, own_dq, new_key_grad, new_value_grad))

    slot_rows = SLOTS * block_rows
    work = 2 * slot_rows * key_rows * LANES * per_group
    wide = pltpu.VMEM((slot_rows, 2 * LANES), BF16)
    slot_stats = pltpu.VMEM((SLOTS, 32, LANES), F32)
    ctx_keys, ctx_values = in_hbm(ctx_keys), in_hbm(ctx_values)
    parts = pl.pallas_call(
        query_kernel,
        out_shape=jax.ShapeDtypeStruct((owners, SLOTS * 32, LANES), BF16),
        in_specs=[smem, vmem(), hbm, hbm],
        out_specs=hbm,
        scratch_shapes=[pltpu.VMEM((per_group, key_rows, LANES), BF16)] * 2
        + [pltpu.VMEM((owners, SLOTS * 32, LANES), BF16), wide, wide, slot_stats]
        + [pltpu.SemaphoreType.DMA((per_group, 2)), pltpu.SemaphoreType.DMA((per_group,))],
        compiler_params=params(28),
        cost_estimate=pl.CostEstimate(flops=8 * work, bytes_accessed=6 << 20, transcendentals=0),
        name="query_parts",
    )(mine, items, ctx_keys, ctx_values)

    returned = lax.all_to_all(parts, "seq", split_axis=0, concat_axis=0, tiled=True)

    later = 3

    def context_grads(first, count, rows_in, grads):
        block = pl.BlockSpec((key_rows, LANES), lambda g: (0, first + g))
        items_spec = pl.BlockSpec((owners, item_rows, LANES), lambda g: (0, 0, 0))
        return pl.pallas_call(
            functools.partial(context_kernel, chunk=256, first=first),
            grid=(count,),
            out_shape=(jax.ShapeDtypeStruct((key_rows, features), BF16),) * 2,
            in_specs=[smem, items_spec, block, block] + [pl.BlockSpec(memory_space=pl.ANY)] * len(grads),
            out_specs=(block, block),
            scratch_shapes=[wide, wide, slot_stats],
            input_output_aliases={4 + n: n for n in range(len(grads))},
            compiler_params=params(24),
            cost_estimate=pl.CostEstimate(flops=10 * work * count // per_group, bytes_accessed=10 << 20, transcendentals=0),
            name="context_grads",
        )(mine, rows_in, ctx_keys, ctx_values, *grads)

    items, _ = lax.optimization_barrier((items, parts))
    grads = context_grads(0, later, items, ())
    returned, grads, items = lax.optimization_barrier((returned, grads, items))
    summed = pl.pallas_call(
        pair_kernel,
        out_shape=jax.ShapeDtypeStruct((owners, 32, LANES), BF16),
        in_specs=[smem, smem, vmem()],
        out_specs=hbm,
        scratch_shapes=[pltpu.VMEM((owners, 32, LANES), BF16), pltpu.SemaphoreType.DMA((4,))],
        compiler_params=params(),
        name="pair_sum",
    )(flat, slot_of * 32, returned)
    home = lax.all_to_all(summed, "seq", split_axis=0, concat_axis=0, tiled=True)
    items, grads, _ = lax.optimization_barrier((items, grads, summed))
    ctx_key_grad, ctx_value_grad = context_grads(later, per_group - later, items, grads)
    query_grad = pl.pallas_call(
        finish_kernel,
        out_shape=jax.ShapeDtypeStruct((block_rows, features), BF16),
        in_specs=[vmem()] * 2,
        out_specs=vmem(),
        compiler_params=params(),
        name="finish",
    )(home, own_dq)
    return (query_grad, new_key_grad, new_value_grad, ctx_key_grad, ctx_value_grad)


def solution(mesh):
    in_specs = (
        P(("seq", "head"), None),
        P(("seq", "head"), None),
        P(("seq", "head"), None),
        P(("seq", "head"), None),
        P(("seq", "head"), None),
        P("head", "seq"),
        P("seq", "head"),
        P("seq", "head"),
        P(),
    )
    out_specs = (P("seq", "head"),) * 5
    return jax.shard_map(per_device, mesh=mesh, in_specs=in_specs, out_specs=out_specs, check_vma=False)
```

```python
import functools
import math

import jax
import jax.numpy as jnp
from jax import lax
from jax.experimental import pallas as pl
from jax.experimental.pallas import tpu as pltpu
from jax.sharding import PartitionSpec as P

BF16 = jnp.bfloat16
F32 = jnp.float32
LANES = 128
MIB = 1024 * 1024
SLOTS = 3
NT = (((1,), (1,)), ((), ()))
TN = (((0,), (0,)), ((), ()))
FILL = 1e5


def dot(lhs, rhs, dims=(((1,), (0,)), ((), ()))):
    return lax.dot_general(lhs, rhs, dims, preferred_element_type=F32)


def vmem():
    return pl.BlockSpec(memory_space=pltpu.VMEM)


def in_hbm(array):
    return pltpu.with_memory_space_constraint(array, pltpu.HBM)


def params(mib=8):
    return pltpu.CompilerParams(vmem_limit_bytes=mib * MIB)


def spread(values, term):
    high = values.astype(BF16)
    low = (values - high.astype(F32)).astype(BF16)
    shape = (values.shape[1], LANES)
    at = lax.broadcasted_iota(jnp.int32, shape, 0) * 4 + term
    lane = lax.broadcasted_iota(jnp.int32, shape, 1)
    out = dot(high, jnp.where(lane == at, 1.0, 0.0).astype(BF16))
    return out + dot(low, jnp.where(lane == at + 1, 1.0, 0.0).astype(BF16))


def statistics_kernel(lse_ref, dots_ref, out_ref):
    out_ref[...] = (spread(lse_ref[...] * math.sqrt(LANES), 0) + spread(dots_ref[...], 2)).astype(BF16)


def prepare_kernel(q_hbm, do_hbm, out_hbm, q_ref, do_ref, out_ref, sems, out_sems, *, per_group):
    copies = [
        pltpu.make_async_copy(src, dst, sems.at[n]) for n, (src, dst) in enumerate(((q_hbm, q_ref), (do_hbm, do_ref)))
    ]
    for copy in copies:
        copy.start()
    rows, features = q_ref.shape
    octets = rows // 8
    heads = features // LANES
    groups = heads // per_group
    leaving = []
    for a, ref in enumerate((q_ref, do_ref)):
        copies[a].wait()
        for g in range(per_group):
            for o in range(octets):
                for h in range(groups):
                    c = (h * per_group + g) * LANES
                    out_ref[((a * per_group + g) * octets + o) * groups + h] = ref[o * 8 : o * 8 + 8, c : c + LANES]
        half = pl.ds(a * per_group * octets * groups, per_group * octets * groups)
        leaving.append(pltpu.make_async_copy(out_ref.at[half], out_hbm.at[half], out_sems.at[a]))
        leaving[a].start()
    for copy in leaving:
        copy.wait()


def dots_kernel(do_ref, o_ref, dots_ref):
    features = do_ref.shape[1]
    heads = features // LANES
    groups, per_group, _ = dots_ref.shape
    product = do_ref[...].astype(F32) * o_ref[...].astype(F32)
    high = product.astype(BF16)
    low = (product - high.astype(F32)).astype(BF16)
    head_at = lax.broadcasted_iota(jnp.int32, (heads, features), 0)
    lane = lax.broadcasted_iota(jnp.int32, (heads, features), 1)
    pick = jnp.where((lane >= head_at * LANES) & (lane < head_at * LANES + LANES), 1.0, 0.0).astype(BF16)
    dots = dot(pick, high, NT) + dot(pick, low, NT)
    for h in range(groups):
        dots_ref[h] = dots[h * per_group : (h + 1) * per_group]


def gather_kernel(src_ref, in_ref, stats_ref, out_hbm, out_ref, sems):
    owners = out_ref.shape[0]
    count = 4

    def leave(part):
        at = pl.ds(part * count, count)
        return pltpu.make_async_copy(out_ref.at[at], out_hbm.at[at], sems.at[part])

    def body(part, carry):
        stats = stats_ref[...]
        for k in range(count):
            j = part * count + k
            for slot in range(SLOTS):
                at = jnp.maximum(src_ref[j * SLOTS + slot], 0)
                out_ref[j, slot * 64 : (slot + 1) * 64, :] = in_ref[at]
            out_ref[j, SLOTS * 64 :, :] = stats
        leave(part).start()
        return carry

    lax.fori_loop(0, owners // count, body, 0)
    for part in range(owners // count):
        leave(part).wait()


def load_statistics(src_ref, x_ref, stats_ref):
    lane = lax.broadcasted_iota(jnp.int32, (32, LANES), 1)
    is_lse = lane % 4 < 2
    for slot in range(SLOTS):
        src = src_ref[slot]
        tile = x_ref[jnp.maximum(src, 0), SLOTS * 64 :, :].astype(F32)
        stats_ref[slot] = jnp.where(is_lse & (src < 0), FILL, tile)


def assemble(x_ref, stats_ref, head, qx, dx):
    row = lax.broadcasted_iota(jnp.int32, (32, LANES), 0)
    lane = lax.broadcasted_iota(jnp.int32, (32, LANES), 1)
    for slot in range(SLOTS):
        stats = stats_ref[slot, pl.ds(pl.multiple_of(head * 8, 8), 8), :]
        for a, out in ((0, qx), (1, dx)):
            first = row * 4 + 2 * a
            mask = (lane == first) | (lane == first + 1)
            for u in range(4):
                base = slot * 256 + u * 64
                out[base : base + 64, 0:LANES] = x_ref[a * 16 + head * 4 + u, slot * 64 : (slot + 1) * 64, :]
            for e in range(8):
                base = slot * 256 + e * 32
                out[base : base + 32, LANES:] = jnp.where(mask, stats[e : e + 1], 0.0).astype(BF16)


def extend(block):
    return jnp.concatenate([block, jnp.full((block.shape[0], LANES), -1.0, BF16)], axis=1)


SCALE = LANES**-0.5
EXP_SCALE = SCALE * math.log2(math.e)


def preload_kernel(k_hbm, v_hbm, k_ref, v_ref, sems):
    at = slice(0, LANES)
    copies = [
        pltpu.make_async_copy(src.at[:, at], dst, sems.at[n]) for n, (src, dst) in enumerate(((k_hbm, k_ref), (v_hbm, v_ref)))
    ]
    for copy in copies:
        copy.start()
    for copy in copies:
        copy.wait()


def query_kernel(src_ref, x_ref, k_near, v_near, k_hbm, v_hbm, out_hbm, k_ref, v_ref, out_ref, qx, dx, stats, sems, out_sems):
    per_group = k_ref.shape[0]

    def fetch(head, which):
        src, dst = ((k_hbm, k_ref), (v_hbm, v_ref))[which]
        at = pl.ds(pl.multiple_of(head * LANES, LANES), LANES)
        return pltpu.make_async_copy(src.at[:, at], dst.at[head], sems.at[head, which])

    def leave(head):
        at = pl.ds(head * 8, 8)
        return pltpu.make_async_copy(out_ref.at[at], out_hbm.at[at], out_sems.at[head])

    fetch(1, 0).start()
    fetch(1, 1).start()
    load_statistics(src_ref, x_ref, stats)

    def work(head, keys, values):
        assemble(x_ref, stats, head, qx, dx)
        keys_ext = extend(keys[...])
        values_ext = extend(values[...])
        for slot in range(SLOTS):
            at = slice(slot * 256, slot * 256 + 256)
            weights = jnp.exp2(dot(qx[at], keys_ext, NT) * EXP_SCALE)
            dscores = (weights * dot(dx[at], values_ext, NT)).astype(BF16)
            part = (dot(dscores, keys[...]) * SCALE).astype(BF16)
            for e in range(8):
                out_ref[head * 8 + e, slot * 32 : (slot + 1) * 32, :] = part[e * 32 : (e + 1) * 32]
        leave(head).start()

    work(0, k_near, v_near)

    def body(head, carry):
        fetch(head, 0).wait()
        fetch(head, 1).wait()

        @pl.when(head + 1 < per_group)
        def _():
            fetch(head + 1, 0).start()
            fetch(head + 1, 1).start()

        work(head, k_ref.at[head], v_ref.at[head])
        return carry

    lax.fori_loop(1, per_group, body, 0)
    for head in range(per_group):
        leave(head).wait()


def context_kernel(src_ref, x_ref, k_ref, v_ref, *refs, chunk, first):
    dk_ref, dv_ref, qx, dx, stats = refs[-5:]
    load_statistics(src_ref, x_ref, stats)
    assemble(x_ref, stats, pl.program_id(0) + first, qx, dx)

    def body(i, carry):
        at = pl.ds(pl.multiple_of(i * chunk, chunk), chunk)
        weights = jnp.exp2(dot(extend(k_ref[at, :]), qx[...], NT) * EXP_SCALE)
        dscores = (weights * dot(extend(v_ref[at, :]), dx[...], NT)).astype(BF16)
        dv_ref[at, :] = dot(weights.astype(BF16), dx[:, 0:LANES]).astype(BF16)
        dk_ref[at, :] = (dot(dscores, qx[:, 0:LANES]) * SCALE).astype(BF16)
        return carry

    lax.fori_loop(0, k_ref.shape[0] // chunk, body, 0, unroll=True)


def own_kernel(me_ref, stats_ref, *refs):
    head = pl.program_id(0)
    window, (dq_ref, dk_ref, dv_ref, qx, dx, kx, vx) = refs[:-7], refs[-7:]
    row = lax.broadcasted_iota(jnp.int32, (8, LANES), 0)
    lane = lax.broadcasted_iota(jnp.int32, (8, LANES), 1)
    stats = stats_ref[0].astype(F32)
    kx[:, LANES:] = jnp.full((kx.shape[0], LANES), -1.0, BF16)
    vx[:, LANES:] = jnp.full((kx.shape[0], LANES), -1.0, BF16)
    for src, w_ref in enumerate(window):
        at = pl.ds(pl.multiple_of((me_ref[0] ^ src) * 32, 32), 32)
        for n, ref in enumerate((qx, dx, kx, vx)):
            piece = pl.ds(pl.multiple_of(n * 128 + head * 32, 32), 32)
            ref[at, 0:LANES] = w_ref[piece, :]
        at = slice(src * 32, src * 32 + 32)
        for a, ref in ((0, qx), (1, dx)):
            first = ((src % 4) * 8 + row) * 4 + 2 * a
            mask = (lane == first) | (lane == first + 1)
            e = src // 4
            terms = [jnp.where(mask, stats[o * 2 + e : o * 2 + e + 1], 0.0) for o in range(4)]
            ref[at, LANES:] = jnp.concatenate(terms, axis=0).astype(BF16)
    shape = (qx.shape[0], kx.shape[0])
    allowed = lax.broadcasted_iota(jnp.int32, shape, 0) >= lax.broadcasted_iota(jnp.int32, shape, 1)
    weights = jnp.where(allowed, jnp.exp2(dot(qx[...], kx[...], NT) * EXP_SCALE), 0.0)
    dscores = (weights * dot(dx[...], vx[...], NT)).astype(BF16)
    dq_ref[...] = dot(dscores, kx[:, 0:LANES]) * SCALE
    dk_ref[...] = (dot(dscores, qx[:, 0:LANES], TN) * SCALE).astype(BF16)
    dv_ref[...] = dot(weights.astype(BF16), dx[:, 0:LANES], TN).astype(BF16)


def pair_kernel(owner_ref, row_ref, in_ref, out_hbm, out_ref, sems):
    count = 8

    def leave(part):
        at = pl.ds(part * count, count)
        return pltpu.make_async_copy(out_ref.at[at], out_hbm.at[at], sems.at[part])

    def body(part, carry):
        for k in range(count):
            b = part * count + k
            total = None
            for s in range(2):
                row = pl.multiple_of(row_ref[b * 2 + s], 32)
                value = in_ref[owner_ref[b * 2 + s], pl.ds(row, 32), :].astype(F32)
                total = value if total is None else total + value
            out_ref[b] = total.astype(BF16)
        leave(part).start()
        return carry

    parts = out_ref.shape[0] // count
    lax.fori_loop(0, parts, body, 0)
    for part in range(parts):
        leave(part).wait()


def finish_kernel(in_ref, own_ref, out_ref):
    for g in range(4):
        at = slice(g * LANES, (g + 1) * LANES)
        parts = [in_ref[g * 8 + e].astype(F32) for e in range(8)]
        for h in range(8):
            octet = slice((h % 4) * 8, (h % 4) * 8 + 8)
            block = jnp.concatenate([parts[o * 2 + h // 4][octet] for o in range(4)], axis=0)
            rows = slice(h * 32, h * 32 + 32)
            out_ref[rows, at] = (block + own_ref[rows, at]).astype(BF16)


def per_device(queries, new_keys, new_values, attn_out, out_grad, logsumexp, ctx_keys, ctx_values, selected):
    owners = lax.axis_size("seq")
    groups = lax.axis_size("head")
    per_group, block_rows = logsumexp.shape
    rows = queries.shape[0]
    key_rows, features = ctx_keys.shape
    relay = lax.axis_index("seq")

    flat = selected.reshape(-1)
    order = jnp.arange(flat.shape[0])
    same = flat[:, None] == flat[None, :]
    slot_of = jnp.sum(same & (order[None, :] < order[:, None]), axis=1).astype(jnp.int32)
    place = flat * SLOTS + slot_of
    hit = place[None, :] == jnp.arange(owners * SLOTS)[:, None]
    source = jnp.max(jnp.where(hit, (order // selected.shape[1])[None, :], -1), axis=1).astype(jnp.int32)
    mine = lax.dynamic_slice(source, (relay * SLOTS,), (SLOTS,))
    me = lax.axis_index("head").astype(jnp.int32)

    def swap(tensor):
        parts = [lax.dynamic_index_in_dim(tensor, me, 0, keepdims=False)]
        for k in range(1, groups):
            part = lax.dynamic_index_in_dim(tensor, me ^ k, 0, keepdims=False)
            parts.append(lax.ppermute(part, "head", [(i, i ^ k) for i in range(groups)]))
        return parts

    hbm = pl.BlockSpec(memory_space=pltpu.HBM)
    smem = pl.BlockSpec(memory_space=pltpu.SMEM)
    tiles = owners * groups
    pieces = pl.pallas_call(
        functools.partial(prepare_kernel, per_group=per_group),
        out_shape=jax.ShapeDtypeStruct((tiles, 8, LANES), BF16),
        in_specs=[hbm] * 2,
        out_specs=hbm,
        scratch_shapes=[pltpu.VMEM(queries.shape, BF16)] * 2
        + [pltpu.VMEM((tiles, 8, LANES), BF16), pltpu.SemaphoreType.DMA((2,)), pltpu.SemaphoreType.DMA((2,))],
        compiler_params=params(),
        name="prepare",
    )(in_hbm(queries), in_hbm(out_grad))
    dots = pl.pallas_call(
        dots_kernel,
        out_shape=jax.ShapeDtypeStruct((groups, per_group, rows), F32),
        in_specs=[vmem()] * 2,
        out_specs=vmem(),
        compiler_params=params(),
        name="out_dot",
    )(*lax.optimization_barrier((out_grad, attn_out, pieces))[:2])
    held = lax.all_to_all(pieces, ("seq", "head"), split_axis=0, concat_axis=0, tiled=True)
    held = held.reshape(owners, 64, LANES)

    dots = jnp.take(jnp.stack(swap(dots)), me ^ jnp.arange(groups), axis=0)
    dots = dots.reshape(2, 4, per_group, 4, 8).transpose(2, 3, 0, 1, 4).reshape(32, 32)
    lse = logsumexp.reshape(per_group, 2, 4, 4, 8).transpose(0, 3, 1, 2, 4).reshape(32, 32)
    stats = pl.pallas_call(
        statistics_kernel,
        out_shape=jax.ShapeDtypeStruct((32, LANES), BF16),
        in_specs=[vmem()] * 2,
        out_specs=vmem(),
        compiler_params=params(),
        name="statistics",
    )(lse, dots)

    item_rows = SLOTS * 64 + 32
    outgoing = pl.pallas_call(
        gather_kernel,
        out_shape=jax.ShapeDtypeStruct((owners, item_rows, LANES), BF16),
        in_specs=[smem, vmem(), vmem()],
        out_specs=hbm,
        scratch_shapes=[pltpu.VMEM((owners, item_rows, LANES), BF16), pltpu.SemaphoreType.DMA((8,))],
        compiler_params=params(),
        name="gather",
    )(source, held, stats)

    window = [
        tensor.reshape(rows, groups, per_group, LANES).transpose(1, 2, 0, 3).reshape(groups, per_group * rows, LANES)
        for tensor in (queries, out_grad, new_keys, new_values)
    ]
    outgoing, window = lax.optimization_barrier((outgoing, jnp.concatenate(window, axis=1)))
    items = lax.all_to_all(outgoing, "seq", split_axis=0, concat_axis=0, tiled=True)
    window = swap(window)

    head_spec = pl.BlockSpec((block_rows, LANES), lambda g: (0, g))
    own_dq, new_key_grad, new_value_grad = pl.pallas_call(
        own_kernel,
        grid=(per_group,),
        out_shape=(
            jax.ShapeDtypeStruct((block_rows, features), F32),
            jax.ShapeDtypeStruct((block_rows, features), BF16),
            jax.ShapeDtypeStruct((block_rows, features), BF16),
        ),
        in_specs=[smem, pl.BlockSpec((1, groups, LANES), lambda g: (g, 0, 0))]
        + [pl.BlockSpec(piece.shape, lambda g: (0, 0)) for piece in window],
        out_specs=(head_spec, head_spec, head_spec),
        scratch_shapes=[pltpu.VMEM((block_rows, 2 * LANES), BF16)] * 4,
        compiler_params=params(),
        cost_estimate=pl.CostEstimate(flops=10 * block_rows * block_rows * features, bytes_accessed=2 << 20, transcendentals=0),
        name="own_set",
    )(me.reshape(1), stats.reshape(per_group, groups, LANES), *window)

    ctx_keys, ctx_values = in_hbm(ctx_keys), in_hbm(ctx_values)
    *near, own_dq, new_key_grad = lax.optimization_barrier((ctx_keys, ctx_values, own_dq, new_key_grad))
    near = pl.pallas_call(
        preload_kernel,
        out_shape=(jax.ShapeDtypeStruct((key_rows, LANES), BF16),) * 2,
        in_specs=[hbm] * 2,
        out_specs=(vmem(), vmem()),
        scratch_shapes=[pltpu.SemaphoreType.DMA((2,))],
        compiler_params=params(),
        name="first_head",
    )(in_hbm(near[0]), in_hbm(near[1]))
    items, near, own_dq, new_key_grad, new_value_grad = lax.optimization_barrier(
        (items, near, own_dq, new_key_grad, new_value_grad)
    )

    slot_rows = SLOTS * block_rows
    work = 2 * slot_rows * key_rows * LANES * per_group
    wide = pltpu.VMEM((slot_rows, 2 * LANES), BF16)
    slot_stats = pltpu.VMEM((SLOTS, 32, LANES), F32)
    parts = pl.pallas_call(
        query_kernel,
        out_shape=jax.ShapeDtypeStruct((owners, SLOTS * 32, LANES), BF16),
        in_specs=[smem, vmem(), vmem(), vmem(), hbm, hbm],
        out_specs=hbm,
        scratch_shapes=[pltpu.VMEM((per_group, key_rows, LANES), BF16)] * 2
        + [pltpu.VMEM((owners, SLOTS * 32, LANES), BF16), wide, wide, slot_stats]
        + [pltpu.SemaphoreType.DMA((per_group, 2)), pltpu.SemaphoreType.DMA((per_group,))],
        compiler_params=params(28),
        cost_estimate=pl.CostEstimate(flops=8 * work, bytes_accessed=6 << 20, transcendentals=0),
        name="query_parts",
    )(mine, items, *near, ctx_keys, ctx_values)

    returned = lax.all_to_all(parts, "seq", split_axis=0, concat_axis=0, tiled=True)

    later = 3

    def context_grads(first, count, rows_in, grads):
        block = pl.BlockSpec((key_rows, LANES), lambda g: (0, first + g))
        items_spec = pl.BlockSpec((owners, item_rows, LANES), lambda g: (0, 0, 0))
        return pl.pallas_call(
            functools.partial(context_kernel, chunk=256, first=first),
            grid=(count,),
            out_shape=(jax.ShapeDtypeStruct((key_rows, features), BF16),) * 2,
            in_specs=[smem, items_spec, block, block] + [pl.BlockSpec(memory_space=pl.ANY)] * len(grads),
            out_specs=(block, block),
            scratch_shapes=[wide, wide, slot_stats],
            input_output_aliases={4 + n: n for n in range(len(grads))},
            compiler_params=params(24),
            cost_estimate=pl.CostEstimate(flops=10 * work * count // per_group, bytes_accessed=10 << 20, transcendentals=0),
            name="context_grads",
        )(mine, rows_in, ctx_keys, ctx_values, *grads)

    items, _ = lax.optimization_barrier((items, parts))
    grads = context_grads(0, later, items, ())
    returned, grads, items = lax.optimization_barrier((returned, grads, items))
    summed = pl.pallas_call(
        pair_kernel,
        out_shape=jax.ShapeDtypeStruct((owners, 32, LANES), BF16),
        in_specs=[smem, smem, vmem()],
        out_specs=hbm,
        scratch_shapes=[pltpu.VMEM((owners, 32, LANES), BF16), pltpu.SemaphoreType.DMA((4,))],
        compiler_params=params(),
        name="pair_sum",
    )(flat, slot_of * 32, returned)
    home = lax.all_to_all(summed, "seq", split_axis=0, concat_axis=0, tiled=True)
    items, grads, _ = lax.optimization_barrier((items, grads, summed))
    ctx_key_grad, ctx_value_grad = context_grads(later, per_group - later, items, grads)
    query_grad = pl.pallas_call(
        finish_kernel,
        out_shape=jax.ShapeDtypeStruct((block_rows, features), BF16),
        in_specs=[vmem()] * 2,
        out_specs=vmem(),
        compiler_params=params(),
        name="finish",
    )(home, own_dq)
    return (query_grad, new_key_grad, new_value_grad, ctx_key_grad, ctx_value_grad)


def solution(mesh):
    in_specs = (
        P(("seq", "head"), None),
        P(("seq", "head"), None),
        P(("seq", "head"), None),
        P(("seq", "head"), None),
        P(("seq", "head"), None),
        P("head", "seq"),
        P("seq", "head"),
        P("seq", "head"),
        P(),
    )
    out_specs = (P("seq", "head"),) * 5
    return jax.shard_map(per_device, mesh=mesh, in_specs=in_specs, out_specs=out_specs, check_vma=False)
```
